512 devices in a mesh: occ: 8 (over y, core), vir: 64 (over x, z).
Axes of the slice: x: 4, y: 4, z: 16, core: 2. Of those that a mesh axis runs over, the one named last changes fastest.
Arguments:
- amplitude: float32 [128, 147456], P('occ', 'vir'), may hold values from -6 to 6
- integrals: float32 [8, 64, 64, 32, 128], P('occ', 'vir'), may hold values from -0.03125 to 0.03125
- task_count: int32 [8, 64], P('occ', 'vir'), may hold values from 1 to 64, 2048 in all within a row
- task_owner: int32 [8, 64, 64, 1], P('occ', 'vir'), may hold values from 0 to 63; in each aligned block of 64 rows (0 to 63, 64 to 127, ..., all dimensions but the last counted through in order) at most 2 rows name the same one
- task_local: int32 [8, 64, 64], P('occ', 'vir'), may hold values from 0 to 17
Outputs:
- ladder: float32 [128, 2048], P('occ', 'vir')
The draws below stay inside these ranges and needn't reach their ends.
Inputs may be any that keep to these rules, and one draw needn't show every extreme that they name: `task_count`: each device has between 1 and 64 live tasks; its live tasks are its first slots, and some device of every index of occ has all 64 live. `task_owner`: among the 64 slots of one device, at most 2 name one index of vir.
All inputs are finite; a program needn't handle non-finite values.
Results may differ from the reference program's by a relative error of at most 0.0003.
Values sent between devices are 32-bit elements; how exact they have to be, the bound alone decides.
A program may use at most 64 MiB of HBM per device.

```python
import math
import jax
import jax.numpy as jnp
import numpy as np
from jax import lax

NV = 384
P_SIZE = 128
TW = 128
KT_DEV = 64
AB_DEV = 32
CT = 1152
TPD = 18
CAP = 2
N_OCC = 8
N_VIR = 64


def plant(array, own_key, low, top_value):
    extent = array.shape
    spot = [jax.random.randint(jax.random.fold_in(own_key, axis), (), 0, extent[axis]) for axis in range(len(extent))]
    array = array.at[tuple(spot)].set(low)
    longest = extent.index(max(extent))
    spot[longest] = (spot[longest] + 1) % extent[longest]
    return array.at[tuple(spot)].set(top_value)


def steps_of(rng, extent, cuts, low, high):
    def one(dim, parts):
        steps = jax.random.uniform(jax.random.fold_in(jax.random.fold_in(rng, 6), dim), (parts,), jnp.float32, low / len(cuts), high / len(cuts))
        return jnp.repeat(jnp.exp(steps), extent[dim] // parts).reshape((-1,) + (1,) * (len(extent) - dim - 1))

    loudness = one(*cuts[0])
    for cut in cuts[1:]:
        loudness = loudness * one(*cut)
    return loudness


def split_up(amount, total, reach, lean):
    portions = [(1 << 20) // math.isqrt(standing ** lean) + 1 for standing in range(2, amount + 1)]
    rest, holding = total - reach - (amount - 1), [1] * (amount - 1)
    while rest > 0:
        candidates = [i for i in range(amount - 1) if holding[i] < reach]
        pool, left = sum([portions[i] for i in candidates]), rest
        for i in candidates:
            extra = min(reach - holding[i], max(1, left * portions[i] // pool), rest)
            holding[i] = holding[i] + extra
            rest = rest - extra
    return np.array([reach] + holding)


def uneven(own_key, count, total, limit, lean):
    if count == 2:
        one = jax.random.randint(own_key, (), max(1, total - limit), min(limit, total - 1) + 1)
        return jnp.stack([one, total - one])
    tallies = jnp.asarray(split_up(count, total, limit, lean), jnp.int32)
    couples = (count - 1) // 2
    donor, receiver = tallies[1:1 + 2 * couples:2], tallies[2:2 + 2 * couples:2]
    room = jnp.minimum(donor - 1, limit - receiver)
    moved = jax.random.randint(jax.random.fold_in(own_key, 1), (couples,), 0, 1 << 20) % (room + 1)
    tallies = tallies.at[1:1 + 2 * couples:2].set(donor - moved).at[2:2 + 2 * couples:2].set(receiver + moved)
    return tallies[jax.random.permutation(jax.random.fold_in(own_key, 2), count)]


def assign_block(own_key, own, number, rows, amount, top, reach, lean):
    order = jax.random.permutation(own_key, amount)
    packed, common = load_shares(amount, rows * top, reach, lean, True), load_shares(amount, rows * top, reach, lean, False)
    places = jnp.arange(amount)

    def named(tallies, offset_by):
        used = int((tallies > 0).sum())
        fixed = max(1, used // 4)
        moved = fixed + (places - fixed + offset_by * (used - fixed)) % max(1, amount - fixed)
        return jnp.zeros((amount,), jnp.int32).at[order[jnp.where(places < fixed, places, moved)]].set(jnp.asarray(tallies, jnp.int32))

    tallies = jnp.where(number % 4 == 0, named(packed, number // 4), named(common, number - number // 4 - 1))
    mixed = jax.random.permutation(jax.random.fold_in(own, 3), amount)
    giver, receiver = mixed[0:amount // 2 * 2:2], mixed[1:amount // 2 * 2:2]
    slack = jnp.minimum(tallies[giver] - 1, reach - tallies[receiver]) // 2
    slack = jnp.where((giver == order[0]) | (receiver == order[0]) | (tallies[receiver] == 0), 0, jnp.maximum(slack, 0))
    moved = jax.random.randint(jax.random.fold_in(own, 4), (amount // 2,), 0, 1 << 20) % (slack + 1)
    tallies = tallies.at[giver].add(-moved).at[receiver].add(moved)
    items = jnp.searchsorted(jnp.cumsum(tallies), jnp.arange(rows * top), side="right").astype(jnp.int32)
    listing = items.reshape(top, rows).T
    listing = listing[jax.random.permutation(jax.random.fold_in(own, 1), rows)]
    offset_by = jax.random.randint(jax.random.fold_in(own, 2), (rows, 1), 0, top)
    return jnp.take_along_axis(listing, (jnp.arange(top)[None, :] + offset_by) % top, axis=1)


def load_shares(amount, total, bound, slope, full):
    portions = [(1 << 20) // math.isqrt(grade ** slope) + 1 for grade in range(1, amount + 1)]
    largest = bound if full else min(bound, max(-(-total // amount), total * portions[0] // sum(portions)))
    least = 1 if total - largest >= amount - 1 else 0
    given, rest = [largest] + [least] * (amount - 1), total - largest - least * (amount - 1)
    while rest > 0:
        movable = [i for i in range(1, amount) if given[i] < largest] or [i for i in range(1, amount) if given[i] < bound]
        mass, left = sum([portions[i] for i in movable]), rest
        for i in movable:
            addition = min(bound - given[i], max(1, left * portions[i] // mass), rest)
            given[i] = given[i] + addition
            rest = rest - addition
    return np.array(given)


def noise(own_key, extent, deviation, limit, pieces=(), kind=jnp.bfloat16):
    values = jax.random.normal(own_key, extent, jnp.float32) * deviation
    if len(pieces) > 0:
        values = steps_of(own_key, extent, pieces, -0.22, 0.18) * values
    return jnp.clip(values, min=-limit, max=limit).astype(kind)


def setup_inputs(seed: int = 0) -> dict:
    streams_of = jax.random.split(jax.random.key(seed), 6)
    amplitude = noise(streams_of[0], (P_SIZE, NV * NV), 1.0, 6.0, ((0, 8), (1, 64)), jnp.float32)
    integrals = noise(streams_of[1], (N_OCC, N_VIR, KT_DEV, AB_DEV, TW), (N_OCC * KT_DEV * TW // 2) ** -0.5, 0.03125, ((0, 8), (1, 64)), jnp.float32)
    task_count = jax.vmap(lambda own: uneven(own, N_VIR, N_VIR * KT_DEV // 2, KT_DEV, 2))(jax.random.split(streams_of[2], N_OCC)).reshape((N_OCC, N_VIR)).astype(jnp.int32)
    task_owner_keys = jax.random.split(jax.random.fold_in(streams_of[3], 1), N_OCC * N_VIR * KT_DEV // KT_DEV)
    task_owner_turns = jax.random.permutation(jax.random.fold_in(streams_of[3], 3), N_OCC * N_VIR * KT_DEV // KT_DEV)
    task_owner = jax.vmap(lambda own, number: assign_block(jax.random.fold_in(streams_of[3], 2), own, number, KT_DEV, N_VIR, 1, CAP, 2))(task_owner_keys, task_owner_turns).reshape((N_OCC, N_VIR, KT_DEV, 1))
    task_local = plant(jax.random.randint(streams_of[4], (N_OCC, N_VIR, KT_DEV), 0, TPD), jax.random.fold_in(streams_of[4], 1), 0, TPD - 1).astype(jnp.int32)
    return {"amplitude": amplitude, "integrals": integrals, "task_count": task_count, "task_owner": task_owner, "task_local": task_local}


def reference(amplitude, integrals, task_count, task_owner, task_local):
    tile_view = amplitude.reshape(P_SIZE, CT, TW)

    def device_term(args):
        int_tiles, count_now, owners, tile_local = args
        tile_ids = (owners[:, 0] * TPD + tile_local).astype(jnp.int32)
        chosen = jnp.take(tile_view, tile_ids, axis=1)
        live_mask = (jnp.arange(KT_DEV, dtype=jnp.int32) < count_now).astype(jnp.float32)
        return jnp.einsum("pkw,kaw->pa", chosen * live_mask[None, :, None], int_tiles,
                          precision=lax.Precision.HIGHEST)

    def occ_row(args):
        return lax.map(device_term, args)

    terms = lax.map(occ_row, (integrals, task_count, task_owner, task_local))
    ladder = jnp.sum(terms, axis=0)
    return jnp.transpose(ladder, (1, 0, 2)).reshape(P_SIZE, N_VIR * AB_DEV)
```

```python
import functools

import jax
import jax.numpy as jnp
from jax import lax
from jax.experimental import pallas as pl
from jax.experimental.pallas import tpu as pltpu
from jax.sharding import PartitionSpec as P

MESH = pl.DeviceIdType.MESH

NX, NY, NZ = 4, 4, 16
PAIRS = 16
TW = 128
TPD = 18
A_TILES = 11
B_TILES = TPD - A_TILES
SLOTS = 64
AB = 32
N_OCC = 8
N_TILES = NX * NZ * TPD
CHUNKS = 4
CHUNK = SLOTS // CHUNKS
GROUP = 8
COPIES = 160


def kernel(amp, ints, ids, out, buf_a, buf_b, buf_i, buf_ids, ids_s, amp_hi, amp_lo, int_hi, int_lo, total,
           own_sem, send_sem, recv_sem):
    o, v = lax.axis_index("occ"), lax.axis_index("vir")
    y, c = o // 2, o % 2
    x, z = v // NZ, v % NZ

    def at(yy, cc, xx, zz):
        return (yy * 2 + cc, xx * NZ + zz)

    xr, xl, xo = (x + 1) % NX, (x + NX - 1) % NX, (x + 2) % NX
    yr, yl, yo = (y + 1) % NY, (y + NY - 1) % NY, (y + 2) % NY
    to_xr, to_xl = at(y, c, xr, z), at(y, c, xl, z)
    to_yr, to_yl = at(yr, c, x, z), at(yl, c, x, z)
    to_zr, to_zl = at(y, c, x, (z + 1) % NZ), at(y, c, x, (z + NZ - 1) % NZ)
    to_co = at(y, 1 - c, x, z)

    own = [
        pltpu.make_async_copy(amp.at[:, pl.ds(0, A_TILES * TW)], buf_a.at[z, x], own_sem.at[0]),
        pltpu.make_async_copy(amp.at[:, pl.ds(A_TILES * TW, B_TILES * TW)], buf_b.at[z, x], own_sem.at[1]),
        pltpu.make_async_copy(ints, buf_i.at[o], own_sem.at[2]),
        pltpu.make_async_copy(ids, buf_ids.at[o], own_sem.at[3]),
    ]
    for copy in own:
        copy.start()

    barrier = pltpu.get_barrier_semaphore()
    for device in (to_xr, to_xl, to_yr, to_yl, to_zr, to_zl, to_co):
        pl.semaphore_signal(barrier, inc=1, device_id=device, device_id_type=MESH)
    pl.semaphore_wait(barrier, 7)

    copies = []

    def send(ref, device):
        n = len(copies)
        copy = pltpu.make_async_remote_copy(
            src_ref=ref, dst_ref=ref, send_sem=send_sem.at[n], recv_sem=recv_sem.at[n],
            device_id=device, device_id_type=MESH,
        )
        copy.start()
        copies.append(copy)
        return copy

    def split(value):
        hi = value.astype(jnp.bfloat16)
        return hi, (value - hi.astype(jnp.float32)).astype(jnp.bfloat16)

    def convert_tiles(buf, zb, xb, first, count):
        def one(t, carry):
            value = buf[zb, xb, :, pl.ds(pl.multiple_of(t * TW, TW), TW)]
            hi, lo = split(value)
            tile = (xb * NZ + zb) * TPD + first + t
            amp_hi[tile] = hi
            amp_lo[tile] = lo
            return carry

        lax.fori_loop(0, count, one, 0)

    def convert_a(zb, xb):
        convert_tiles(buf_a, zb, xb, 0, A_TILES)

    def convert_b(zb):
        def one(xb, carry):
            convert_tiles(buf_b, zb, xb, A_TILES, B_TILES)
            return carry

        lax.fori_loop(0, NX, one, 0)

    def convert_ints(oo, q):
        def one(t, carry):
            hi, lo = split(buf_i[oo, q * CHUNK + t])
            int_hi[oo * SLOTS + q * CHUNK + t] = hi
            int_lo[oo * SLOTS + q * CHUNK + t] = lo
            return carry

        lax.fori_loop(0, CHUNK, one, 0)

    top, bottom = pl.ds(0, PAIRS // 2), pl.ds(PAIRS // 2, PAIRS // 2)

    order = [z]
    for s in range(1, NZ // 2):
        order += [(z + NZ - s) % NZ, (z + s) % NZ]
    order.append((z + NZ // 2) % NZ)
    ring_a = {}

    def a_send(s):
        if s == 0:
            right, left = buf_a.at[z, x], buf_a.at[z, x]
        else:
            right, left = buf_a.at[order[2 * s - 1], x], buf_a.at[order[2 * s], x]
        if s == NZ // 2 - 1:
            right = buf_a.at[order[2 * s - 1], x, top]
            left = buf_a.at[order[2 * s], x, bottom]
        ring_a[s] = send(right, to_zr), send(left, to_zl)

    def a_step(s):
        for copy in ring_a[s]:
            copy.wait_recv()
        if s < NZ // 2 - 1:
            a_send(s + 1)

    full_x, half_x = {}, {}

    def x_issue(i):
        block = buf_a.at[order[i], x]
        full_x[i] = send(block, to_xr), send(block, to_xl)

    def x_forward(i):
        full_x[i][0].wait_recv()
        right = send(buf_a.at[order[i], xl, top], to_xr)
        full_x[i][1].wait_recv()
        half_x[i] = right, send(buf_a.at[order[i], xr, bottom], to_xl)
        for xb in (x, xl, xr):
            convert_a(order[i], xb)

    def x_finish(i):
        for copy in half_x[i]:
            copy.wait_recv()
        convert_a(order[i], xo)

    state_b = {}

    def b_issue():
        state_b["full"] = send(buf_b.at[z, x], to_xr), send(buf_b.at[z, x], to_xl)

    def b_forward():
        state_b["full"][0].wait_recv()
        right = send(buf_b.at[z, xl, top], to_xr)
        state_b["full"][1].wait_recv()
        state_b["half"] = right, send(buf_b.at[z, xr, bottom], to_xl)

    def b_finish():
        for copy in state_b["half"]:
            copy.wait_recv()
        b_send(0)
        convert_b(z)

    ring_b = {}

    def b_send(s):
        if s == 0:
            right, left = z, z
        else:
            right, left = order[2 * s - 1], order[2 * s]
        ring_b[s] = []
        for first in (0, 2):
            if s == NZ // 2 - 1:
                ring_b[s] += [send(buf_b.at[right, pl.ds(first, 1)], to_zr), send(buf_b.at[left, pl.ds(first + 1, 1)], to_zl)]
            else:
                ring_b[s] += [send(buf_b.at[right, pl.ds(first, 2)], to_zr), send(buf_b.at[left, pl.ds(first, 2)], to_zl)]

    def b_step(s):
        for copy in ring_b[s]:
            copy.wait_recv()
        if s < NZ // 2 - 1:
            b_send(s + 1)
            convert_b(order[2 * s + 1])
            convert_b(order[2 * s + 2])
        else:
            convert_b(order[NZ - 1])

    def line(yy, cc):
        return yy * 2 + cc

    full_i, half_i, core_i = {}, {}, {}

    def piece(oo, first, count):
        return buf_i.at[oo, pl.ds(first, count)]

    def i_issue(q):
        block = piece(o, q * CHUNK, CHUNK)
        full_i[q] = send(block, to_yr), send(block, to_yl)
        core_i[q] = [send(block, to_co)]

    def i_forward(q):
        full_i[q][0].wait_recv()
        right = send(piece(line(yl, c), q * CHUNK, CHUNK // 2), to_yr)
        core_i[q].append(send(piece(line(yl, c), q * CHUNK, CHUNK), to_co))
        full_i[q][1].wait_recv()
        half_i[q] = right, send(piece(line(yr, c), q * CHUNK + CHUNK // 2, CHUNK // 2), to_yl)
        core_i[q].append(send(piece(line(yr, c), q * CHUNK, CHUNK), to_co))
        for yy in (y, yl, yr):
            convert_ints(line(yy, c), q)

    def i_finish(q):
        for copy in half_i[q]:
            copy.wait_recv()
        core_i[q].append(send(piece(line(yo, c), q * CHUNK, CHUNK), to_co))
        convert_ints(line(yo, c), q)

    def i_core(q):
        for copy in core_i[q]:
            copy.wait_recv()
        for yy in range(NY):
            convert_ints(line(yy, 1 - c), q)

    def ids_issue():
        block = buf_ids.at[o]
        return [send(block, to_yr), send(block, to_yl), send(block, to_co)]

    def ids_forward(sent):
        sent[0].wait_recv()
        sent[1].wait_recv()
        return [
            send(buf_ids.at[line(yl, c)], to_yr),
            send(buf_ids.at[line(yl, c)], to_co),
            send(buf_ids.at[line(yr, c)], to_co),
        ]

    for copy in own:
        copy.wait()
    a_send(0)
    b_issue()
    x_issue(0)
    ids_sent = ids_issue()
    for q in range(CHUNKS):
        i_issue(q)
    amp_hi[N_TILES] = jnp.zeros((PAIRS, TW), jnp.bfloat16)
    amp_lo[N_TILES] = jnp.zeros((PAIRS, TW), jnp.bfloat16)
    total[...] = jnp.zeros_like(total)

    a_at = {0: 0, 2: 1, 3: 2, 5: 3, 6: 4, 8: 5, 9: 6, 11: 7}
    b_at = {4: 0, 7: 1, 10: 2, 12: 3, 13: 4, 15: 5, 16: 6, 17: 7}
    i_at = {3: 0, 5: 1, 7: 2, 9: 3}
    f_at = {6: 0, 8: 1, 10: 2, 12: 3}
    k_at = {9: 0, 11: 1, 13: 2, 15: 3}
    ids_all = []
    for it in range(18):
        if it in a_at:
            a_step(a_at[it])
        if it == 0:
            b_forward()
        if 1 <= it < 16:
            x_issue(it)
        if it == 1:
            b_finish()
            ids_all = ids_forward(ids_sent)
        if 1 <= it < 17:
            x_forward(it - 1)
        if 2 <= it:
            x_finish(it - 2)
        if it == 2:
            ids_all[0].wait_recv()
            ids_all.append(send(buf_ids.at[line(yo, c)], to_co))
        if it in b_at:
            b_step(b_at[it])
        if it in i_at:
            i_forward(i_at[it])
        if it in f_at:
            i_finish(f_at[it])
        if it in k_at:
            i_core(k_at[it])
        if it == 8:
            for copy in [ids_sent[2]] + ids_all[1:]:
                copy.wait_recv()
            load = pltpu.make_async_copy(buf_ids, ids_s, own_sem.at[4])
            load.start()
            load.wait()

    def tiles(ref, g):
        oo, first = g // (SLOTS // GROUP), (g % (SLOTS // GROUP)) * GROUP
        return jnp.concatenate([ref[ids_s[oo, 0, first + j]] for j in range(GROUP)], axis=0)

    def rows(ref, g):
        return ref[pl.ds(g * GROUP, GROUP)].reshape(GROUP * AB, TW)

    def dot(a, b):
        return lax.dot_general(a, b, (((1,), (1,)), ((), ())), preferred_element_type=jnp.float32)

    def product(h, carry):
        g = 2 * h
        a_hi = jnp.concatenate([tiles(amp_hi, g), tiles(amp_hi, g + 1)], axis=1)
        a_lo = jnp.concatenate([tiles(amp_lo, g), tiles(amp_lo, g + 1)], axis=1)
        b_hi = jnp.concatenate([rows(int_hi, g), rows(int_hi, g + 1)], axis=1)
        b_lo = jnp.concatenate([rows(int_lo, g), rows(int_lo, g + 1)], axis=1)
        total[...] += dot(a_hi, b_hi) + dot(a_lo, b_hi) + dot(a_hi, b_lo)
        return carry

    lax.fori_loop(0, N_OCC * SLOTS // GROUP // 2, product, 0)
    result = total[pl.ds(0, PAIRS), pl.ds(0, AB)]
    for j in range(1, GROUP):
        result = result + total[pl.ds(j * PAIRS, PAIRS), pl.ds(j * AB, AB)]
    out[...] = result
    for copy in copies:
        copy.wait_send()


def body(amplitude, integrals, task_count, task_owner, task_local):
    live = jnp.arange(SLOTS, dtype=jnp.int32) < task_count[0, 0]
    ids = jnp.where(live, task_owner[0, 0, :, 0] * TPD + task_local[0, 0], N_TILES)
    ids = jnp.broadcast_to(jnp.pad(ids, (0, TW - SLOTS))[None, :], (8, TW))
    f32, bf16 = jnp.float32, jnp.bfloat16
    return pl.pallas_call(
        kernel,
        out_shape=jax.ShapeDtypeStruct((PAIRS, AB), f32),
        in_specs=[pl.BlockSpec(memory_space=pl.ANY)] * 3,
        out_specs=pl.BlockSpec(memory_space=pltpu.VMEM),
        scratch_shapes=[
            pltpu.VMEM((NZ, NX, PAIRS, A_TILES * TW), f32),
            pltpu.VMEM((NZ, NX, PAIRS, B_TILES * TW), f32),
            pltpu.VMEM((N_OCC, SLOTS, AB, TW), f32),
            pltpu.VMEM((N_OCC, 8, TW), jnp.int32),
            pltpu.SMEM((N_OCC, 8, TW), jnp.int32),
            pltpu.VMEM((N_TILES + 1, PAIRS, TW), bf16),
            pltpu.VMEM((N_TILES + 1, PAIRS, TW), bf16),
            pltpu.VMEM((N_OCC * SLOTS, AB, TW), bf16),
            pltpu.VMEM((N_OCC * SLOTS, AB, TW), bf16),
            pltpu.VMEM((GROUP * PAIRS, GROUP * AB), f32),
            pltpu.SemaphoreType.DMA((5,)),
            pltpu.SemaphoreType.DMA((COPIES,)),
            pltpu.SemaphoreType.DMA((COPIES,)),
        ],
        compiler_params=pltpu.CompilerParams(
            collective_id=0, has_side_effects=True, vmem_limit_bytes=48 * 1024 * 1024
        ),
    )(amplitude, integrals[0, 0], ids)


def solution(mesh):
    in_specs = (
        P("occ", "vir"),
        P("occ", "vir", None, None, None),
        P("occ", "vir"),
        P("occ", "vir", None, None),
        P("occ", "vir", None),
    )
    return jax.shard_map(body, mesh=mesh, in_specs=in_specs, out_specs=P("occ", "vir"), check_vma=False)
```

```python
import jax
import jax.numpy as jnp
from jax import lax
from jax.experimental import pallas as pl
from jax.experimental.pallas import tpu as pltpu
from jax.sharding import PartitionSpec as P

MESH = pl.DeviceIdType.MESH

NX, NY, NZ = 4, 4, 16
PAIRS = 16
TW = 128
TPD = 18
SLOTS = 64
AB = 32
N_OCC = 8
N_TILES = NX * NZ * TPD
GROUP = 8
N_GROUPS = N_OCC * SLOTS // GROUP
DEPTH = 4

PARTS = 3
LAG = 5
TABLE = (
    (128, 64, 0, -1, -1, 65, 79, 15, 80, 16, 81, 14, 142, 2, 31, 77, 94, 67, 141, 18, 93, 76, 147, 157, 140, 68, 148, 4, 75, 11,
     69, 74, 149, 181, 27, 5, 90, 150, 137, 54, 70, 26, 102, 153, 25, 82, 138, 158, 95, -1),
    (64, 128, 0, -1, -1, 79, 176, 15, 129, 1, 66, 78, 14, 130, 2, 77, 67, 191, 62, 178, 68, 115, 140, 12, 61, 116, 51, 75, 188,
     60, 69, 74, 123, 187, 10, 53, 73, 186, 150, 54, 137, 72, 121, 136, 55, 151, 148, 141, 49, -1),
    (64, 0, 128, -1, -1, 65, 144, 129, 1, 16, 66, 145, 81, 2, 160, 67, 146, 130, 178, 50, 3, 147, 18, 179, 51, 68, 4, 148, 180,
     52, 100, 35, 149, 69, 53, 181, 101, 150, 70, 54, 182, 102, 166, 21, 55, 86, 103, 167, 22, -1),
    (64, 0, 128, -1, -1, 79, 15, 143, 144, 176, 78, 95, 142, 14, 191, 77, 30, 141, 13, 62, 125, 76, 29, 140, 12, 109, 75, 188,
     139, 11, 156, 74, 187, 138, 27, 10, 73, 90, 137, 26, 9, 58, 89, 153, 25, 8, 120, 60, 114, 41),
)
STEPS = len(TABLE[0])
PT = TPD // PARTS
STEP_OF = ((0, 0, 0), (1, 1, 0), (2, 0, 1), (3, 0, -1))

Y_TASKS = 4
Y_OWN = SLOTS // Y_TASKS
Y_MSGS = Y_OWN + Y_OWN // 2
Y_STEP = [m * (STEPS - 12) // Y_MSGS for m in range(Y_MSGS)]
BATCH = 4
COPIES = 4 * STEPS + 2 * Y_MSGS + 24


def kernel(amp, ints, count_hbm, owner_hbm, local_hbm, out, buf_a, buf_i, buf_ids, ids_s, count_s, owner_v, local_v,
           amp_hi, amp_lo, int_hi, int_lo, total, own_sem, send_sem, recv_sem):
    o, v = lax.axis_index("occ"), lax.axis_index("vir")
    y, c = o // 2, o % 2
    x, z = v // NZ, v % NZ

    def at(yy, cc, xx, zz):
        return (yy * 2 + cc, xx * NZ + zz)

    def line(yy, cc):
        return yy * 2 + cc

    yr, yl, yo = (y + 1) % NY, (y + NY - 1) % NY, (y + 2) % NY
    to_yr, to_yl = at(yr, c, x, z), at(yl, c, x, z)
    to_co = at(y, 1 - c, x, z)
    to = (
        at(y, c, (x + 1) % NX, z),
        at(y, c, (x + NX - 1) % NX, z),
        at(y, c, x, (z + 1) % NZ),
        at(y, c, x, (z + NZ - 1) % NZ),
    )

    own = [
        pltpu.make_async_copy(count_hbm, count_s, own_sem.at[0]),
        pltpu.make_async_copy(owner_hbm, owner_v, own_sem.at[1]),
        pltpu.make_async_copy(local_hbm, local_v, own_sem.at[2]),
        pltpu.make_async_copy(ints, buf_i.at[o], own_sem.at[3]),
    ]
    for p in range(PARTS):
        own.append(pltpu.make_async_copy(amp.at[:, pl.ds(p * PT * TW, PT * TW)], buf_a.at[p, z, x], own_sem.at[4 + p]))
    for copy in own:
        copy.start()

    barrier = pltpu.get_barrier_semaphore()
    for device in (to_yr, to_yl, to_co) + to:
        pl.semaphore_signal(barrier, inc=1, device_id=device, device_id_type=MESH)

    copies = []

    def send(ref, device):
        n = len(copies)
        copy = pltpu.make_async_remote_copy(
            src_ref=ref, dst_ref=ref, send_sem=send_sem.at[n], recv_sem=recv_sem.at[n],
            device_id=device, device_id_type=MESH,
        )
        copy.start()
        copies.append(copy)
        return copy

    def split(value):
        hi = value.astype(jnp.bfloat16)
        return hi, (value - hi.astype(jnp.float32)).astype(jnp.bfloat16)

    def place(code):
        p, dx, dz = code // 64, code // NZ % NX, code % NZ
        return p, (z + NZ - dz) % NZ, (x + NX - dx) % NX

    def convert_part(p, zb, xb):
        first = (xb * NZ + zb) * TPD + p * PT

        def one(t, carry):
            hi, lo = split(buf_a[p, zb, xb, :, pl.ds(pl.multiple_of(t * TW, TW), TW)])
            amp_hi[first + t] = hi
            amp_lo[first + t] = lo
            return carry

        lax.fori_loop(0, PT, one, 0)

    def convert_groups(oo, first, number):
        def one(j, carry):
            rows = buf_i[oo, pl.ds((first + j) * GROUP, GROUP)].reshape(GROUP * AB, TW)
            hi, lo = split(rows.T)
            g = oo * (SLOTS // GROUP) + first + j
            int_hi[g] = hi
            int_lo[g] = lo
            return carry

        lax.fori_loop(0, number, one, 0)

    def tasks(oo, m, number):
        return buf_i.at[oo, pl.ds(m * Y_TASKS, number * Y_TASKS)]

    for copy in own[:3]:
        copy.wait()
    slot = lax.broadcasted_iota(jnp.int32, (1, SLOTS), 1)
    ids = jnp.where(slot < count_s[0, 0], owner_v[...] * TPD + local_v[...], N_TILES)
    buf_ids[o] = jnp.zeros((8, TW), jnp.int32)
    buf_ids[o, :, pl.ds(0, SLOTS)] = jnp.broadcast_to(ids, (8, SLOTS))
    for copy in own[3:]:
        copy.wait()
    pl.semaphore_wait(barrier, 7)

    sent, sent_y, sent_co, sent_ids = {}, {}, [], []
    todo = {}

    def later(t, work):
        todo.setdefault(t, []).append(work)

    def to_core(t, oo, m, number):
        copy = send(tasks(oo, m, number), to_co)
        other = oo + 1 - 2 * c

        def work():
            copy.wait_recv()
            convert_groups(other, m * Y_TASKS // GROUP, number * Y_TASKS // GROUP)

        later(t + LAG, work)

    def y_arrived(t, m):
        for copy in sent_y[m]:
            copy.wait_recv()
        end = m + 1
        if end % BATCH:
            return
        first = end - BATCH
        groups = BATCH * Y_TASKS // GROUP
        if m < Y_OWN:
            for yy in (yl, yr):
                to_core(t, line(yy, c), first, BATCH)
                convert_groups(line(yy, c), first * Y_TASKS // GROUP, groups)
        else:
            for half in (0, Y_OWN // 2):
                to_core(t, line(yo, c), half + first - Y_OWN, BATCH)
                convert_groups(line(yo, c), (half + first - Y_OWN) * Y_TASKS // GROUP, groups)

    def y_send(m):
        if m < Y_OWN:
            block = tasks(o, m, 1)
            sent_y[m] = send(block, to_yr), send(block, to_yl)
        else:
            k = m - Y_OWN
            sent_y[m] = send(tasks(line(yl, c), k, 1), to_yr), send(tasks(line(yr, c), Y_OWN // 2 + k, 1), to_yl)

    for t in range(STEPS + 3 * LAG):
        if LAG <= t < STEPS + LAG:
            for copy in sent[t - LAG].values():
                copy.wait_recv()
        if t < STEPS:
            sent[t] = {}
            for d in range(4):
                if TABLE[d][t] >= 0:
                    p, zb, xb = place(TABLE[d][t])
                    sent[t][d] = send(buf_a.at[p, zb, xb], to[d])
        for m in range(Y_MSGS):
            if Y_STEP[m] == t:
                y_send(m)
        if t == 0:
            block = buf_ids.at[o]
            sent_ids = [send(block, to_yr), send(block, to_yl), send(block, to_co)]
            amp_hi[N_TILES] = jnp.zeros((PAIRS, TW), jnp.bfloat16)
            amp_lo[N_TILES] = jnp.zeros((PAIRS, TW), jnp.bfloat16)
            total[...] = jnp.zeros_like(total)
            for p in range(PARTS):
                convert_part(p, z, x)
        if t == 1:
            for q in range(0, Y_OWN, BATCH):
                to_core(t, o, q, BATCH)
            convert_groups(o, 0, SLOTS // GROUP)
        if t == LAG:
            sent_ids[0].wait_recv()
            sent_ids[1].wait_recv()
            sent_ids += [
                send(buf_ids.at[line(yl, c)], to_yr),
                send(buf_ids.at[line(yl, c)], to_co),
                send(buf_ids.at[line(yr, c)], to_co),
            ]
        if t == 2 * LAG:
            sent_ids[3].wait_recv()
            sent_ids.append(send(buf_ids.at[line(yo, c)], to_co))
        if t == 3 * LAG:
            for copy in [sent_ids[2]] + sent_ids[4:]:
                copy.wait_recv()
            load = pltpu.make_async_copy(buf_ids, ids_s, own_sem.at[0])
            load.start()
            load.wait()
        for m in range(Y_MSGS):
            if Y_STEP[m] + LAG == t:
                y_arrived(t, m)
        for work in todo.pop(t, []):
            work()
        if LAG <= t < STEPS + LAG:
            for d, dx, dz in STEP_OF:
                if TABLE[d][t - LAG] >= 0:
                    p, zb, xb = place(TABLE[d][t - LAG])
                    if d == 0:
                        xb = (xb + NX - 1) % NX
                    elif d == 1:
                        xb = (xb + 1) % NX
                    elif d == 2:
                        zb = (zb + NZ - 1) % NZ
                    else:
                        zb = (zb + 1) % NZ
                    convert_part(p, zb, xb)

    def tiles(ref, g):
        oo, first = g // (SLOTS // GROUP), (g % (SLOTS // GROUP)) * GROUP
        return jnp.concatenate([ref[ids_s[oo, 0, first + j]] for j in range(GROUP)], axis=0)

    def dot(a, b):
        return lax.dot_general(a, b, (((1,), (0,)), ((), ())), preferred_element_type=jnp.float32)

    def product(h, carry):
        g = DEPTH * h
        a_hi = jnp.concatenate([tiles(amp_hi, g + j) for j in range(DEPTH)], axis=1)
        a_lo = jnp.concatenate([tiles(amp_lo, g + j) for j in range(DEPTH)], axis=1)
        b_hi = int_hi[pl.ds(g, DEPTH)].reshape(DEPTH * TW, GROUP * AB)
        b_lo = int_lo[pl.ds(g, DEPTH)].reshape(DEPTH * TW, GROUP * AB)
        total[...] += dot(a_hi, b_hi) + dot(a_lo, b_hi) + dot(a_hi, b_lo)
        return carry

    lax.fori_loop(0, N_GROUPS // DEPTH, product, 0)
    result = total[pl.ds(0, PAIRS), pl.ds(0, AB)]
    for j in range(1, GROUP):
        result = result + total[pl.ds(j * PAIRS, PAIRS), pl.ds(j * AB, AB)]
    out[...] = result
    for copy in copies:
        copy.wait_send()


def body(amplitude, integrals, task_count, task_owner, task_local):
    f32, bf16 = jnp.float32, jnp.bfloat16
    return pl.pallas_call(
        kernel,
        out_shape=jax.ShapeDtypeStruct((PAIRS, AB), f32),
        in_specs=[pl.BlockSpec(memory_space=pltpu.HBM)] * 5,
        out_specs=pl.BlockSpec(memory_space=pltpu.VMEM),
        scratch_shapes=[
            pltpu.VMEM((PARTS, NZ, NX, PAIRS, PT * TW), f32),
            pltpu.VMEM((N_OCC, SLOTS, AB, TW), f32),
            pltpu.VMEM((N_OCC, 8, TW), jnp.int32),
            pltpu.SMEM((N_OCC, 8, TW), jnp.int32),
            pltpu.SMEM((1, 1), jnp.int32),
            pltpu.VMEM((1, SLOTS), jnp.int32),
            pltpu.VMEM((1, SLOTS), jnp.int32),
            pltpu.VMEM((N_TILES + 1, PAIRS, TW), bf16),
            pltpu.VMEM((N_TILES + 1, PAIRS, TW), bf16),
            pltpu.VMEM((N_GROUPS, TW, GROUP * AB), bf16),
            pltpu.VMEM((N_GROUPS, TW, GROUP * AB), bf16),
            pltpu.VMEM((GROUP * PAIRS, GROUP * AB), f32),
            pltpu.SemaphoreType.DMA((4 + PARTS,)),
            pltpu.SemaphoreType.DMA((COPIES,)),
            pltpu.SemaphoreType.DMA((COPIES,)),
        ],
        compiler_params=pltpu.CompilerParams(
            collective_id=0, has_side_effects=True, vmem_limit_bytes=64 * 1024 * 1024
        ),
    )(
        amplitude,
        integrals[0, 0],
        task_count,
        task_owner.reshape(1, SLOTS),
        task_local.reshape(1, SLOTS),
    )


def solution(mesh):
    in_specs = (
        P("occ", "vir"),
        P("occ", "vir", None, None, None),
        P("occ", "vir"),
        P("occ", "vir", None, None),
        P("occ", "vir", None),
    )
    return jax.shard_map(body, mesh=mesh, in_specs=in_specs, out_specs=P("occ", "vir"), check_vma=False)
```

```python
import jax
import jax.numpy as jnp
from jax import lax
from jax.experimental import pallas as pl
from jax.experimental.pallas import tpu as pltpu
from jax.sharding import PartitionSpec as P

MESH = pl.DeviceIdType.MESH

NX, NY, NZ = 4, 4, 16
PAIRS = 16
TW = 128
TPD = 18
SLOTS = 64
AB = 32
N_OCC = 8
N_TILES = NX * NZ * TPD
GROUP = 8
N_GROUPS = N_OCC * SLOTS // GROUP
DEPTH = 16

PARTS = 3
LAGS = (3, 3, 3, 4, 4, 4, 5,)
LAG = LAGS[-1]
TABLE = (
    (128, 64, 0, 144, 1, 143, 65, 129, 15, 130, 159, 14, 77, 18, 146, 67, 131, 30, 13, 76, 19, 147, 12, 4, 29, 84, 140, 28, 5, 74,
     139, 69, 20, 6, 134, 155, 21, 9, 7, 71, 135, 22, 25, 136, 23, 100, 31, -1),
    (64, 128, 0, 79, 112, 1, 48, 15, 78, 130, 127, 49, 77, 14, 190, 113, 67, 125, 3, 114, 189, 13, 12, 4, 75, 124, 188, 69, 11,
     74, 5, 181, 10, 117, 59, 122, 70, 58, 9, 121, 7, 185, 183, 186, 120, 180, 129, -1),
    (64, 0, 128, 112, 65, 129, 1, 160, 17, 49, 66, 130, 2, 113, 178, 18, 67, 3, 131, 179, 83, 68, 4, 132, 147, 98, 180, 5, 133,
     69, 148, 181, 6, 134, 70, 53, 182, 165, 135, 101, 71, 183, 118, 25, 102, 85, 81, -1),
    (64, 0, 128, 79, 176, 80, 15, 78, 143, 191, 95, 159, 14, 142, 77, 190, 158, 13, 141, 76, 125, 189, 12, 140, 75, 92, 188, 11,
     28, 74, 108, 187, 10, 139, 122, 90, 186, 155, 138, 121, 89, 9, 25, 154, 57, 111, 169, 41),
)
STEPS = len(TABLE[0])
PT = TPD // PARTS

Y_TASKS = 4
Y_OWN = SLOTS // Y_TASKS
Y_MSGS = Y_OWN + Y_OWN // 2
Y_STEP = [m * (STEPS - 12) // Y_MSGS for m in range(Y_MSGS)]
BATCH = 4
SEND_AGAIN, RECV_AGAIN = 7, 13
Y_SEND_AGAIN, Y_RECV_AGAIN = 6, 9
SINGLES = 24


def lag(t):
    return LAGS[min(t, len(LAGS) - 1)]


def kernel(amp, ints, count_hbm, owner_hbm, local_hbm, out, buf_a, buf_i, buf_ids, ids_s, count_s, owner_v, local_v,
           amp_hi, amp_lo, int_hi, int_lo, total, own_sem, send_sem, recv_sem,
           y_send_sem, y_recv_sem, one_send_sem, one_recv_sem):
    o, v = lax.axis_index("occ"), lax.axis_index("vir")
    y, c = o // 2, o % 2
    x, z = v // NZ, v % NZ

    def at(yy, cc, xx, zz):
        return (yy * 2 + cc, xx * NZ + zz)

    def line(yy, cc):
        return yy * 2 + cc

    yr, yl, yo = (y + 1) % NY, (y + NY - 1) % NY, (y + 2) % NY
    to_yr, to_yl = at(yr, c, x, z), at(yl, c, x, z)
    to_co = at(y, 1 - c, x, z)
    to = (
        at(y, c, (x + 1) % NX, z),
        at(y, c, (x + NX - 1) % NX, z),
        at(y, c, x, (z + 1) % NZ),
        at(y, c, x, (z + NZ - 1) % NZ),
    )

    own = [
        pltpu.make_async_copy(count_hbm, count_s, own_sem.at[0]),
        pltpu.make_async_copy(owner_hbm, owner_v, own_sem.at[1]),
        pltpu.make_async_copy(local_hbm, local_v, own_sem.at[2]),
        pltpu.make_async_copy(ints, buf_i.at[o], own_sem.at[3]),
    ]
    for p in range(PARTS):
        own.append(pltpu.make_async_copy(amp.at[:, pl.ds(p * PT * TW, PT * TW)], buf_a.at[p, z, x], own_sem.at[4 + p]))
    for copy in own:
        copy.start()

    barrier = pltpu.get_barrier_semaphore()
    for device in (to_yr, to_yl, to_co) + to:
        pl.semaphore_signal(barrier, inc=1, device_id=device, device_id_type=MESH)

    def start(ref, device, send_one, recv_one):
        copy = pltpu.make_async_remote_copy(
            src_ref=ref, dst_ref=ref, send_sem=send_one, recv_sem=recv_one, device_id=device, device_id_type=MESH
        )
        copy.start()
        return copy

    singles = []

    def send(ref, device):
        n = len(singles)
        singles.append(start(ref, device, one_send_sem.at[n], one_recv_sem.at[n]))
        return singles[n]

    def split(value):
        hi = value.astype(jnp.bfloat16)
        return hi, (value - hi.astype(jnp.float32)).astype(jnp.bfloat16)

    def place(code):
        p, dx, dz = code // 64, code // NZ % NX, code % NZ
        return p, (z + NZ - dz) % NZ, (x + NX - dx) % NX

    def convert_part(p, zb, xb):
        first = (xb * NZ + zb) * TPD + p * PT

        def one(t, carry):
            hi, lo = split(buf_a[p, zb, xb, :, pl.ds(pl.multiple_of(t * TW, TW), TW)])
            amp_hi[first + t] = hi
            amp_lo[first + t] = lo
            return carry

        lax.fori_loop(0, PT, one, 0)

    def convert_groups(oo, first, number):
        def one(j, carry):
            rows = buf_i[oo, pl.ds((first + j) * GROUP, GROUP)].reshape(GROUP * AB, TW)
            hi, lo = split(rows.T)
            g = oo * (SLOTS // GROUP) + first + j
            int_hi[g] = hi
            int_lo[g] = lo
            return carry

        lax.fori_loop(0, number, one, 0)

    def tasks(oo, m, number):
        return buf_i.at[oo, pl.ds(m * Y_TASKS, number * Y_TASKS)]

    for copy in own[:3]:
        copy.wait()
    slot = lax.broadcasted_iota(jnp.int32, (1, SLOTS), 1)
    ids = jnp.where(slot < count_s[0, 0], owner_v[...] * TPD + local_v[...], N_TILES)
    buf_ids[o] = jnp.zeros((8, TW), jnp.int32)
    buf_ids[o, :, pl.ds(0, SLOTS)] = jnp.broadcast_to(ids, (8, SLOTS))
    for copy in own[3:]:
        copy.wait()
    pl.semaphore_wait(barrier, 7)

    sent, sent_y, sent_co, sent_ids = {}, {}, [], []
    todo = {}

    def later(t, work):
        todo.setdefault(t, []).append(work)

    def to_core(t, oo, m, number):
        copy = send(tasks(oo, m, number), to_co)
        other = oo + 1 - 2 * c

        def work():
            copy.wait_recv()
            convert_groups(other, m * Y_TASKS // GROUP, number * Y_TASKS // GROUP)

        later(t + LAG, work)

    def y_arrived(t, m):
        for copy in sent_y[m]:
            copy.wait_recv()
        end = m + 1
        if end % BATCH:
            return
        first = end - BATCH
        groups = BATCH * Y_TASKS // GROUP
        if m < Y_OWN:
            for yy in (yl, yr):
                to_core(t, line(yy, c), first, BATCH)
                convert_groups(line(yy, c), first * Y_TASKS // GROUP, groups)
        else:
            for half in (0, Y_OWN // 2):
                to_core(t, line(yo, c), half + first - Y_OWN, BATCH)
                convert_groups(line(yo, c), (half + first - Y_OWN) * Y_TASKS // GROUP, groups)

    def y_send(m):
        if m >= Y_SEND_AGAIN:
            for copy in sent_y[m - Y_SEND_AGAIN]:
                copy.wait_send()
        if m < Y_OWN:
            right = left = tasks(o, m, 1)
        else:
            right = tasks(line(yl, c), m - Y_OWN, 1)
            left = tasks(line(yr, c), Y_OWN // 2 + m - Y_OWN, 1)
        sent_y[m] = [
            start(ref, device, y_send_sem.at[d, m % Y_SEND_AGAIN], y_recv_sem.at[d, m % Y_RECV_AGAIN])
            for d, (ref, device) in enumerate(((right, to_yr), (left, to_yl)))
        ]

    for t in range(STEPS + 3 * LAG):
        arrived = [s for s in range(STEPS) if s + lag(s) == t]
        for s in arrived:
            for copy in sent[s].values():
                copy.wait_recv()
        if t < STEPS:
            for copy in sent.get(t - SEND_AGAIN, {}).values():
                copy.wait_send()
            sent[t] = {}
            for d in range(4):
                if TABLE[d][t] >= 0:
                    p, zb, xb = place(TABLE[d][t])
                    sent[t][d] = start(
                        buf_a.at[p, zb, xb], to[d], send_sem.at[d, t % SEND_AGAIN], recv_sem.at[d, t % RECV_AGAIN]
                    )
        for m in range(Y_MSGS):
            if Y_STEP[m] == t:
                y_send(m)
        if t == 0:
            block = buf_ids.at[o]
            sent_ids = [send(block, to_yr), send(block, to_yl), send(block, to_co)]
            amp_hi[N_TILES] = jnp.zeros((PAIRS, TW), jnp.bfloat16)
            amp_lo[N_TILES] = jnp.zeros((PAIRS, TW), jnp.bfloat16)
            total[...] = jnp.zeros_like(total)
            for p in range(PARTS):
                convert_part(p, z, x)
        if t == 1:
            for q in range(0, Y_OWN, BATCH):
                to_core(t, o, q, BATCH)
            convert_groups(o, 0, SLOTS // GROUP)
        if t == LAG:
            sent_ids[0].wait_recv()
            sent_ids[1].wait_recv()
            sent_ids += [
                send(buf_ids.at[line(yl, c)], to_yr),
                send(buf_ids.at[line(yl, c)], to_co),
                send(buf_ids.at[line(yr, c)], to_co),
            ]
        if t == 2 * LAG:
            sent_ids[3].wait_recv()
            sent_ids.append(send(buf_ids.at[line(yo, c)], to_co))
        if t == 3 * LAG:
            for copy in [sent_ids[2]] + sent_ids[4:]:
                copy.wait_recv()
            load = pltpu.make_async_copy(buf_ids, ids_s, own_sem.at[0])
            load.start()
            load.wait()
        for m in range(Y_MSGS):
            if Y_STEP[m] + LAG == t:
                y_arrived(t, m)
        for work in todo.pop(t, []):
            work()
        for s in arrived:
            for d in range(4):
                if TABLE[d][s] >= 0:
                    p, zb, xb = place(TABLE[d][s])
                    if d == 0:
                        xb = (xb + NX - 1) % NX
                    elif d == 1:
                        xb = (xb + 1) % NX
                    elif d == 2:
                        zb = (zb + NZ - 1) % NZ
                    else:
                        zb = (zb + 1) % NZ
                    convert_part(p, zb, xb)

    def tiles(ref, g):
        oo, first = g // (SLOTS // GROUP), (g % (SLOTS // GROUP)) * GROUP
        return jnp.concatenate([ref[ids_s[oo, 0, first + j]] for j in range(GROUP)], axis=0)

    def dot(a, b):
        return lax.dot_general(a, b, (((1,), (0,)), ((), ())), preferred_element_type=jnp.float32)

    def product(h, carry):
        g = DEPTH * h
        a_hi = jnp.concatenate([tiles(amp_hi, g + j) for j in range(DEPTH)], axis=1)
        a_lo = jnp.concatenate([tiles(amp_lo, g + j) for j in range(DEPTH)], axis=1)
        b_hi = int_hi[pl.ds(g, DEPTH)].reshape(DEPTH * TW, GROUP * AB)
        b_lo = int_lo[pl.ds(g, DEPTH)].reshape(DEPTH * TW, GROUP * AB)
        total[...] += dot(a_hi, b_hi) + dot(a_lo, b_hi) + dot(a_hi, b_lo)
        return carry

    lax.fori_loop(0, N_GROUPS // DEPTH, product, 0)
    result = total[pl.ds(0, PAIRS), pl.ds(0, AB)]
    for j in range(1, GROUP):
        result = result + total[pl.ds(j * PAIRS, PAIRS), pl.ds(j * AB, AB)]
    out[...] = result
    left = [copy for t in range(STEPS - SEND_AGAIN, STEPS) for copy in sent[t].values()]
    left += [copy for m in range(Y_MSGS - Y_SEND_AGAIN, Y_MSGS) for copy in sent_y[m]]
    for copy in left + singles:
        copy.wait_send()


def body(amplitude, integrals, task_count, task_owner, task_local):
    f32, bf16 = jnp.float32, jnp.bfloat16
    return pl.pallas_call(
        kernel,
        out_shape=jax.ShapeDtypeStruct((PAIRS, AB), f32),
        in_specs=[pl.BlockSpec(memory_space=pltpu.HBM)] * 5,
        out_specs=pl.BlockSpec(memory_space=pltpu.VMEM),
        scratch_shapes=[
            pltpu.VMEM((PARTS, NZ, NX, PAIRS, PT * TW), f32),
            pltpu.VMEM((N_OCC, SLOTS, AB, TW), f32),
            pltpu.VMEM((N_OCC, 8, TW), jnp.int32),
            pltpu.SMEM((N_OCC, 8, TW), jnp.int32),
            pltpu.SMEM((1, 1), jnp.int32),
            pltpu.VMEM((1, SLOTS), jnp.int32),
            pltpu.VMEM((1, SLOTS), jnp.int32),
            pltpu.VMEM((N_TILES + 1, PAIRS, TW), bf16),
            pltpu.VMEM((N_TILES + 1, PAIRS, TW), bf16),
            pltpu.VMEM((N_GROUPS, TW, GROUP * AB), bf16),
            pltpu.VMEM((N_GROUPS, TW, GROUP * AB), bf16),
            pltpu.VMEM((GROUP * PAIRS, GROUP * AB), f32),
            pltpu.SemaphoreType.DMA((4 + PARTS,)),
            pltpu.SemaphoreType.DMA((4, SEND_AGAIN)),
            pltpu.SemaphoreType.DMA((4, RECV_AGAIN)),
            pltpu.SemaphoreType.DMA((2, Y_SEND_AGAIN)),
            pltpu.SemaphoreType.DMA((2, Y_RECV_AGAIN)),
            pltpu.SemaphoreType.DMA((SINGLES,)),
            pltpu.SemaphoreType.DMA((SINGLES,)),
        ],
        compiler_params=pltpu.CompilerParams(
            collective_id=0, has_side_effects=True, vmem_limit_bytes=64 * 1024 * 1024
        ),
    )(
        amplitude,
        integrals[0, 0],
        task_count,
        task_owner.reshape(1, SLOTS),
        task_local.reshape(1, SLOTS),
    )


def solution(mesh):
    in_specs = (
        P("occ", "vir"),
        P("occ", "vir", None, None, None),
        P("occ", "vir"),
        P("occ", "vir", None, None),
        P("occ", "vir", None),
    )
    return jax.shard_map(body, mesh=mesh, in_specs=in_specs, out_specs=P("occ", "vir"), check_vma=False)
```

```python
import jax
import jax.numpy as jnp
from jax import lax
from jax.experimental import pallas as pl
from jax.experimental.pallas import tpu as pltpu
from jax.sharding import PartitionSpec as P

MESH = pl.DeviceIdType.MESH

NX, NY, NZ = 4, 4, 16
PAIRS = 16
TW = 128
TPD = 18
SLOTS = 64
AB = 32
N_OCC = 8
N_TILES = NX * NZ * TPD
GROUP = 8
N_GROUPS = N_OCC * SLOTS // GROUP

PARTS = 3
LAGS = (3, 3, 3, 4, 4, 4, 5,)
LAG = LAGS[-1]
TABLE = (
    (128, 64, 0, 144, 1, 143, 65, 129, 15, 130, 159, 14, 77, 18, 146, 67, 131, 30, 13, 76, 19, 147, 12, 4, 29, 84, 140, 28, 5, 74,
     139, 69, 20, 6, 134, 155, 21, 9, 7, 71, 135, 22, 25, 136, 23, 100, 31, -1),
    (64, 128, 0, 79, 112, 1, 48, 15, 78, 130, 127, 49, 77, 14, 190, 113, 67, 125, 3, 114, 189, 13, 12, 4, 75, 124, 188, 69, 11,
     74, 5, 181, 10, 117, 59, 122, 70, 58, 9, 121, 7, 185, 183, 186, 120, 180, 129, -1),
    (64, 0, 128, 112, 65, 129, 1, 160, 17, 49, 66, 130, 2, 113, 178, 18, 67, 3, 131, 179, 83, 68, 4, 132, 147, 98, 180, 5, 133,
     69, 148, 181, 6, 134, 70, 53, 182, 165, 135, 101, 71, 183, 118, 25, 102, 85, 81, -1),
    (64, 0, 128, 79, 176, 80, 15, 78, 143, 191, 95, 159, 14, 142, 77, 190, 158, 13, 141, 76, 125, 189, 12, 140, 75, 92, 188, 11,
     28, 74, 108, 187, 10, 139, 122, 90, 186, 155, 138, 121, 89, 9, 25, 154, 57, 111, 169, 41),
)
STEPS = len(TABLE[0])
PT = TPD // PARTS

Y_TASKS = 4
Y_OWN = SLOTS // Y_TASKS
Y_MSGS = Y_OWN + Y_OWN // 2
Y_STEP = [m * (STEPS - 12) // Y_MSGS for m in range(Y_MSGS)]
BATCH = 4
SEND_AGAIN, RECV_AGAIN = 7, 13
Y_SEND_AGAIN, Y_RECV_AGAIN = 6, 9
SINGLES = 24


def lag(t):
    return LAGS[min(t, len(LAGS) - 1)]


def kernel(amp, ints, count_hbm, owner_hbm, local_hbm, out, buf_a, buf_i, buf_ids, ids_s, count_s, owner_v, local_v,
           amp_hi, amp_lo, int_hi, int_lo, total, own_sem, send_sem, recv_sem,
           y_send_sem, y_recv_sem, one_send_sem, one_recv_sem):
    o, v = lax.axis_index("occ"), lax.axis_index("vir")
    y, c = o // 2, o % 2
    x, z = v // NZ, v % NZ

    def at(yy, cc, xx, zz):
        return (yy * 2 + cc, xx * NZ + zz)

    def line(yy, cc):
        return yy * 2 + cc

    yr, yl, yo = (y + 1) % NY, (y + NY - 1) % NY, (y + 2) % NY
    to_yr, to_yl = at(yr, c, x, z), at(yl, c, x, z)
    to_co = at(y, 1 - c, x, z)
    to = (
        at(y, c, (x + 1) % NX, z),
        at(y, c, (x + NX - 1) % NX, z),
        at(y, c, x, (z + 1) % NZ),
        at(y, c, x, (z + NZ - 1) % NZ),
    )

    own = [
        pltpu.make_async_copy(count_hbm, count_s, own_sem.at[0]),
        pltpu.make_async_copy(owner_hbm, owner_v, own_sem.at[1]),
        pltpu.make_async_copy(local_hbm, local_v, own_sem.at[2]),
        pltpu.make_async_copy(ints, buf_i.at[o], own_sem.at[3]),
    ]
    for p in range(PARTS):
        own.append(pltpu.make_async_copy(amp.at[:, pl.ds(p * PT * TW, PT * TW)], buf_a.at[p, z, x], own_sem.at[4 + p]))
    for copy in own:
        copy.start()

    barrier = pltpu.get_barrier_semaphore()
    for device in (to_yr, to_yl, to_co) + to:
        pl.semaphore_signal(barrier, inc=1, device_id=device, device_id_type=MESH)

    def start(ref, device, send_one, recv_one, source=None):
        copy = pltpu.make_async_remote_copy(
            src_ref=ref if source is None else source, dst_ref=ref, send_sem=send_one, recv_sem=recv_one, device_id=device, device_id_type=MESH
        )
        copy.start()
        return copy

    singles = []

    def send(ref, device, source=None):
        n = len(singles)
        singles.append(start(ref, device, one_send_sem.at[n], one_recv_sem.at[n], source))
        return singles[n]

    def split(value):
        hi = value.astype(jnp.bfloat16)
        return hi, (value - hi.astype(jnp.float32)).astype(jnp.bfloat16)

    def place(code):
        p, dx, dz = code // 64, code // NZ % NX, code % NZ
        return p, (z + NZ - dz) % NZ, (x + NX - dx) % NX

    def convert_part(p, zb, xb):
        first = (xb * NZ + zb) * TPD + p * PT

        def one(t, carry):
            hi, lo = split(buf_a[p, zb, xb, :, pl.ds(pl.multiple_of(t * TW, TW), TW)])
            amp_hi[first + t] = hi
            amp_lo[first + t] = lo
            return carry

        lax.fori_loop(0, PT, one, 0)

    def convert_groups(oo, first, number):
        def one(j, carry):
            rows = buf_i[oo, pl.ds((first + j) * GROUP, GROUP)].reshape(GROUP * AB, TW)
            hi, lo = split(rows.T)
            g = oo * (SLOTS // GROUP) + first + j
            int_hi[g] = hi
            int_lo[g] = lo
            return carry

        lax.fori_loop(0, number, one, 0)

    def tasks(oo, m, number):
        return buf_i.at[oo, pl.ds(m * Y_TASKS, number * Y_TASKS)]

    pl.semaphore_wait(barrier, 7)

    def number_tasks():
        for copy in own[:3]:
            copy.wait()
        slot = lax.broadcasted_iota(jnp.int32, (1, SLOTS), 1)
        ids = jnp.where(slot < count_s[0, 0], owner_v[...] * TPD + local_v[...], N_TILES)
        buf_ids[o] = jnp.zeros((8, TW), jnp.int32)
        buf_ids[o, :, pl.ds(0, SLOTS)] = jnp.broadcast_to(ids, (8, SLOTS))

    sent, sent_y, sent_co, sent_ids = {}, {}, [], []
    todo = {}

    def later(t, work):
        todo.setdefault(t, []).append(work)

    def to_core(t, oo, m, number, source=None):
        copy = send(tasks(oo, m, number), to_co, source)
        other = oo + 1 - 2 * c

        def work():
            copy.wait_recv()
            convert_groups(other, m * Y_TASKS // GROUP, number * Y_TASKS // GROUP)

        later(t + LAG, work)

    def y_arrived(t, m):
        for copy in sent_y[m]:
            copy.wait_recv()
        end = m + 1
        if end % BATCH:
            return
        first = end - BATCH
        groups = BATCH * Y_TASKS // GROUP
        if m < Y_OWN:
            for yy in (yl, yr):
                to_core(t, line(yy, c), first, BATCH)
                convert_groups(line(yy, c), first * Y_TASKS // GROUP, groups)
        else:
            for half in (0, Y_OWN // 2):
                to_core(t, line(yo, c), half + first - Y_OWN, BATCH)
                convert_groups(line(yo, c), (half + first - Y_OWN) * Y_TASKS // GROUP, groups)

    def y_send(m):
        if m >= Y_SEND_AGAIN:
            for copy in sent_y[m - Y_SEND_AGAIN]:
                copy.wait_send()
        if m < Y_OWN:
            right = left = tasks(o, m, 1)
            source = ints.at[pl.ds(m * Y_TASKS, Y_TASKS)]
        else:
            source = None
            right = tasks(line(yl, c), m - Y_OWN, 1)
            left = tasks(line(yr, c), Y_OWN // 2 + m - Y_OWN, 1)
        sent_y[m] = [
            start(ref, device, y_send_sem.at[d, m % Y_SEND_AGAIN], y_recv_sem.at[d, m % Y_RECV_AGAIN], source)
            for d, (ref, device) in enumerate(((right, to_yr), (left, to_yl)))
        ]

    for t in range(STEPS + 3 * LAG):
        arrived = [s for s in range(STEPS) if s + lag(s) == t]
        for s in arrived:
            for copy in sent[s].values():
                copy.wait_recv()
        if t < STEPS:
            for copy in sent.get(t - SEND_AGAIN, {}).values():
                copy.wait_send()
            sent[t] = {}
            for d in range(4):
                if TABLE[d][t] >= 0:
                    p, zb, xb = place(TABLE[d][t])
                    mine = amp.at[:, pl.ds(p * PT * TW, PT * TW)] if TABLE[d][t] % 64 == 0 else None
                    sent[t][d] = start(
                        buf_a.at[p, zb, xb], to[d], send_sem.at[d, t % SEND_AGAIN], recv_sem.at[d, t % RECV_AGAIN], mine
                    )
        for m in range(Y_MSGS):
            if Y_STEP[m] == t:
                y_send(m)
        if t == 0:
            number_tasks()
            block = buf_ids.at[o]
            sent_ids = [send(block, to_yr), send(block, to_yl), send(block, to_co)]
            amp_hi[N_TILES] = jnp.zeros((PAIRS, TW), jnp.bfloat16)
            amp_lo[N_TILES] = jnp.zeros((PAIRS, TW), jnp.bfloat16)
            for copy in own[4:]:
                copy.wait()
            for p in range(PARTS):
                convert_part(p, z, x)
        if t == 1:
            for q in range(0, Y_OWN, BATCH):
                to_core(t, o, q, BATCH, ints.at[pl.ds(q * Y_TASKS, BATCH * Y_TASKS)])
            own[3].wait()
            convert_groups(o, 0, SLOTS // GROUP)
        if t == LAG:
            sent_ids[0].wait_recv()
            sent_ids[1].wait_recv()
            sent_ids += [
                send(buf_ids.at[line(yl, c)], to_yr),
                send(buf_ids.at[line(yl, c)], to_co),
                send(buf_ids.at[line(yr, c)], to_co),
            ]
        if t == 2 * LAG:
            sent_ids[3].wait_recv()
            sent_ids.append(send(buf_ids.at[line(yo, c)], to_co))
        if t == 3 * LAG:
            for copy in [sent_ids[2]] + sent_ids[4:]:
                copy.wait_recv()
            load = pltpu.make_async_copy(buf_ids, ids_s, own_sem.at[0])
            load.start()
            load.wait()
        for m in range(Y_MSGS):
            if Y_STEP[m] + LAG == t:
                y_arrived(t, m)
        for work in todo.pop(t, []):
            work()
        for s in arrived:
            for d in range(4):
                if TABLE[d][s] >= 0:
                    p, zb, xb = place(TABLE[d][s])
                    if d == 0:
                        xb = (xb + NX - 1) % NX
                    elif d == 1:
                        xb = (xb + 1) % NX
                    elif d == 2:
                        zb = (zb + NZ - 1) % NZ
                    else:
                        zb = (zb + 1) % NZ
                    convert_part(p, zb, xb)

    def tiles(ref, g):
        oo, first = g // (SLOTS // GROUP), (g % (SLOTS // GROUP)) * GROUP
        return jnp.concatenate([ref[ids_s[oo, 0, first + j]] for j in range(GROUP)], axis=0)

    def dot(a, b):
        return lax.dot_general(a, b, (((1,), (0,)), ((), ())), preferred_element_type=jnp.float32)

    a_hi = jnp.concatenate([tiles(amp_hi, g) for g in range(N_GROUPS)], axis=1)
    a_lo = jnp.concatenate([tiles(amp_lo, g) for g in range(N_GROUPS)], axis=1)
    b_hi = int_hi[...].reshape(N_GROUPS * TW, GROUP * AB)
    b_lo = int_lo[...].reshape(N_GROUPS * TW, GROUP * AB)
    total[...] = dot(a_hi, b_hi) + dot(a_lo, b_hi) + dot(a_hi, b_lo)
    result = total[pl.ds(0, PAIRS), pl.ds(0, AB)]
    for j in range(1, GROUP):
        result = result + total[pl.ds(j * PAIRS, PAIRS), pl.ds(j * AB, AB)]
    out[...] = result
    left = [copy for t in range(STEPS - SEND_AGAIN, STEPS) for copy in sent[t].values()]
    left += [copy for m in range(Y_MSGS - Y_SEND_AGAIN, Y_MSGS) for copy in sent_y[m]]
    for copy in left + singles:
        copy.wait_send()


def body(amplitude, integrals, task_count, task_owner, task_local):
    f32, bf16 = jnp.float32, jnp.bfloat16
    return pl.pallas_call(
        kernel,
        out_shape=jax.ShapeDtypeStruct((PAIRS, AB), f32),
        in_specs=[pl.BlockSpec(memory_space=pltpu.HBM)] * 5,
        out_specs=pl.BlockSpec(memory_space=pltpu.VMEM),
        scratch_shapes=[
            pltpu.VMEM((PARTS, NZ, NX, PAIRS, PT * TW), f32),
            pltpu.VMEM((N_OCC, SLOTS, AB, TW), f32),
            pltpu.VMEM((N_OCC, 8, TW), jnp.int32),
            pltpu.SMEM((N_OCC, 8, TW), jnp.int32),
            pltpu.SMEM((1, 1), jnp.int32),
            pltpu.VMEM((1, SLOTS), jnp.int32),
            pltpu.VMEM((1, SLOTS), jnp.int32),
            pltpu.VMEM((N_TILES + 1, PAIRS, TW), bf16),
            pltpu.VMEM((N_TILES + 1, PAIRS, TW), bf16),
            pltpu.VMEM((N_GROUPS, TW, GROUP * AB), bf16),
            pltpu.VMEM((N_GROUPS, TW, GROUP * AB), bf16),
            pltpu.VMEM((GROUP * PAIRS, GROUP * AB), f32),
            pltpu.SemaphoreType.DMA((4 + PARTS,)),
            pltpu.SemaphoreType.DMA((4, SEND_AGAIN)),
            pltpu.SemaphoreType.DMA((4, RECV_AGAIN)),
            pltpu.SemaphoreType.DMA((2, Y_SEND_AGAIN)),
            pltpu.SemaphoreType.DMA((2, Y_RECV_AGAIN)),
            pltpu.SemaphoreType.DMA((SINGLES,)),
            pltpu.SemaphoreType.DMA((SINGLES,)),
        ],
        compiler_params=pltpu.CompilerParams(
            collective_id=0, has_side_effects=True, vmem_limit_bytes=64 * 1024 * 1024
        ),
    )(
        amplitude,
        integrals[0, 0],
        task_count,
        task_owner.reshape(1, SLOTS),
        task_local.reshape(1, SLOTS),
    )


def solution(mesh):
    in_specs = (
        P("occ", "vir"),
        P("occ", "vir", None, None, None),
        P("occ", "vir"),
        P("occ", "vir", None, None),
        P("occ", "vir", None),
    )
    return jax.shard_map(body, mesh=mesh, in_specs=in_specs, out_specs=P("occ", "vir"), check_vma=False)
```

```python
import jax
import jax.numpy as jnp
from jax import lax
from jax.experimental import pallas as pl
from jax.experimental.pallas import tpu as pltpu
from jax.sharding import PartitionSpec as P

MESH = pl.DeviceIdType.MESH

NX, NY, NZ = 4, 4, 16
PAIRS = 16
TW = 128
TPD = 18
SLOTS = 64
AB = 32
N_OCC = 8
N_TILES = NX * NZ * TPD
GROUP = 8
N_GROUPS = N_OCC * SLOTS // GROUP

PARTS = 3
LAGS = (3, 3, 3, 4, 4, 5, 5, 5,)
LAG = LAGS[-1]
TABLE = (
    (0, 128, 64, 16, 144, 1, 143, 14, 130, 78, 142, 2, 30, 3, 13, 67, 141, 4, 132, 76, 68, 157, 140, 147, 11, 133, 139, 10, 69,
     91, 149, 74, 7, 135, 73, 71, 27, 25, 72, 89, 19, 158, 81, 175, 88, 23, 87, -1),
    (64, 0, 128, 112, 79, 65, 129, 2, 14, 127, 142, 177, 66, 131, 77, 141, 3, 114, 76, 125, 68, 140, 11, 75, 60, 116, 52, 6, 134,
     74, 70, 138, 54, 182, 187, 137, 135, 8, 136, 72, 185, 61, 1, 126, 184, 122, 183, 102),
    (0, 128, 64, 1, 129, 65, 80, 2, 130, 32, 66, 177, 3, 131, 81, 67, 146, 4, 132, 179, 68, 51, 5, 133, 180, 69, 52, 6, 134, 20,
     70, 100, 7, 135, 54, 118, 101, 33, 46, 151, 161, 144, 62, 36, 114, 41, 149, -1),
    (0, 64, 128, 15, 79, 143, 16, 14, 78, 127, 142, 160, 13, 77, 62, 141, 94, 12, 76, 61, 140, 29, 11, 75, 92, 139, 188, 10, 74,
     59, 138, 155, 26, 73, 58, 122, 154, 25, 100, 109, 173, 80, 165, 118, 41, 23, 171, -1),
)
STEPS = len(TABLE[0])
PT = TPD // PARTS
LATE_STEPS = 3
LATE = ((1, 6), (2, 7), (2, 10))
CAP = 2
LATE_TASKS = CAP * len(LATE)
LATE_GROUPS = N_OCC * LATE_TASKS // GROUP

Y_TASKS = 4
Y_OWN = SLOTS // Y_TASKS
Y_MSGS = Y_OWN + Y_OWN // 2
Y_STEP = [m * (STEPS - 12) // Y_MSGS for m in range(Y_MSGS)]
BATCH = 4
SEND_AGAIN, RECV_AGAIN = 6, 12
Y_SEND_AGAIN, Y_RECV_AGAIN = 6, 9
SINGLES = 23
LATE_READY = Y_STEP[-1] + 2 * LAG


def lag(t):
    return LAGS[min(t, len(LAGS) - 1)]


def kernel(amp, ints, count_hbm, owner_hbm, local_hbm, out, buf_a, buf_i, buf_ids, ids_s, count_s, owner_v, local_v,
           amp_hi, amp_lo, int_hi, int_lo, late_hi, late_lo, lists, late_task_s, late_tile_s, total, own_sem, send_sem, recv_sem,
           y_send_sem, y_recv_sem, one_send_sem, one_recv_sem):
    o, v = lax.axis_index("occ"), lax.axis_index("vir")
    y, c = o // 2, o % 2
    x, z = v // NZ, v % NZ

    def at(yy, cc, xx, zz):
        return (yy * 2 + cc, xx * NZ + zz)

    def line(yy, cc):
        return yy * 2 + cc

    yr, yl, yo = (y + 1) % NY, (y + NY - 1) % NY, (y + 2) % NY
    to_yr, to_yl = at(yr, c, x, z), at(yl, c, x, z)
    to_co = at(y, 1 - c, x, z)
    to = (
        at(y, c, (x + 1) % NX, z),
        at(y, c, (x + NX - 1) % NX, z),
        at(y, c, x, (z + 1) % NZ),
        at(y, c, x, (z + NZ - 1) % NZ),
    )

    own = [
        pltpu.make_async_copy(count_hbm, count_s, own_sem.at[0]),
        pltpu.make_async_copy(owner_hbm, owner_v, own_sem.at[1]),
        pltpu.make_async_copy(local_hbm, local_v, own_sem.at[2]),
        pltpu.make_async_copy(ints, buf_i.at[o], own_sem.at[3]),
    ]
    for p in range(PARTS):
        own.append(pltpu.make_async_copy(amp.at[:, pl.ds(p * PT * TW, PT * TW)], buf_a.at[p, z, x], own_sem.at[4 + p]))
    for copy in own:
        copy.start()

    barrier = pltpu.get_barrier_semaphore()
    for device in (to_yr, to_yl, to_co) + to:
        pl.semaphore_signal(barrier, inc=1, device_id=device, device_id_type=MESH)

    def start(ref, device, send_one, recv_one, source=None):
        copy = pltpu.make_async_remote_copy(
            src_ref=ref if source is None else source, dst_ref=ref, send_sem=send_one, recv_sem=recv_one, device_id=device, device_id_type=MESH
        )
        copy.start()
        return copy

    singles = []

    def send(ref, device, source=None):
        n = len(singles)
        singles.append(start(ref, device, one_send_sem.at[n], one_recv_sem.at[n], source))
        return singles[n]

    def split(value):
        hi = value.astype(jnp.bfloat16)
        return hi, (value - hi.astype(jnp.float32)).astype(jnp.bfloat16)

    def place(code):
        p, dx, dz = code // 64, code // NZ % NX, code % NZ
        return p, (z + NZ - dz) % NZ, (x + NX - dx) % NX

    def convert_part(p, zb, xb):
        first = (xb * NZ + zb) * TPD + p * PT

        def one(t, carry):
            hi, lo = split(buf_a[p, zb, xb, :, pl.ds(pl.multiple_of(t * TW, TW), TW)])
            amp_hi[first + t] = hi
            amp_lo[first + t] = lo
            return carry

        lax.fori_loop(0, PT, one, 0, unroll=True)

    def convert_groups(oo, first, number):
        def one(j, carry):
            rows = buf_i[oo, pl.ds((first + j) * GROUP, GROUP)].reshape(GROUP * AB, TW)
            hi, lo = split(rows.T)
            g = oo * (SLOTS // GROUP) + first + j
            int_hi[g] = hi
            int_lo[g] = lo
            return carry

        lax.fori_loop(0, number, one, 0)

    def tasks(oo, m, number):
        return buf_i.at[oo, pl.ds(m * Y_TASKS, number * Y_TASKS)]

    pl.semaphore_wait(barrier, 7)

    def number_tasks():
        for copy in own[:3]:
            copy.wait()
        slot = lax.broadcasted_iota(jnp.int32, (1, SLOTS), 1)
        ids = jnp.where(slot < count_s[0, 0], owner_v[...] * TPD + local_v[...], N_TILES)
        buf_ids[o] = jnp.zeros((8, TW), jnp.int32)
        buf_ids[o, :, pl.ds(0, SLOTS)] = jnp.broadcast_to(ids, (8, SLOTS))

    sent, sent_y, sent_co, sent_ids = {}, {}, [], []
    todo = {}

    def later(t, work):
        todo.setdefault(t, []).append(work)

    def to_core(t, oo, m, number, source=None):
        copy = send(tasks(oo, m, number), to_co, source)
        other = oo + 1 - 2 * c

        def work():
            copy.wait_recv()
            convert_groups(other, m * Y_TASKS // GROUP, number * Y_TASKS // GROUP)

        later(t + LAG, work)

    def y_arrived(t, m):
        for copy in sent_y[m]:
            copy.wait_recv()
        end = m + 1
        if end % BATCH:
            return
        first = end - BATCH
        groups = BATCH * Y_TASKS // GROUP
        if m < Y_OWN:
            for yy in (yl, yr):
                to_core(t, line(yy, c), first, BATCH)
                convert_groups(line(yy, c), first * Y_TASKS // GROUP, groups)
        else:
            for half in (0, Y_OWN // 2):
                to_core(t, line(yo, c), half + first - Y_OWN, BATCH)
                convert_groups(line(yo, c), (half + first - Y_OWN) * Y_TASKS // GROUP, groups)

    def y_send(m):
        if m >= Y_SEND_AGAIN:
            for copy in sent_y[m - Y_SEND_AGAIN]:
                copy.wait_send()
        if m < Y_OWN:
            right = left = tasks(o, m, 1)
            source = ints.at[pl.ds(m * Y_TASKS, Y_TASKS)]
        else:
            source = None
            right = tasks(line(yl, c), m - Y_OWN, 1)
            left = tasks(line(yr, c), Y_OWN // 2 + m - Y_OWN, 1)
        sent_y[m] = [
            start(ref, device, y_send_sem.at[d, m % Y_SEND_AGAIN], y_recv_sem.at[d, m % Y_RECV_AGAIN], source)
            for d, (ref, device) in enumerate(((right, to_yr), (left, to_yl)))
        ]

    def list_tasks():
        ids = jnp.concatenate([buf_ids[oo, pl.ds(0, 1), :] for oo in range(N_OCC)], axis=0)
        lane = lax.broadcasted_iota(jnp.int32, (N_OCC, TW), 1)
        early, late_task, late_tile = ids, jnp.zeros((N_OCC, TW), jnp.int32), jnp.full((N_OCC, TW), N_TILES, jnp.int32)
        for j, (dx, dz) in enumerate(LATE):
            first = ((x + NX - dx) % NX * NZ + (z + NZ - dz) % NZ) * TPD
            named = (ids >= first) & (ids < first + TPD) & (lane < SLOTS)
            early = jnp.where(named, N_TILES, early)
            low = jnp.min(jnp.where(named, lane, TW), axis=1, keepdims=True)
            high = jnp.max(jnp.where(named, lane, -1), axis=1, keepdims=True)
            for r, (task, there) in enumerate(((low, low < TW), (high, high > low))):
                tile = jnp.sum(jnp.where(named & (lane == task), ids, 0), axis=1, keepdims=True)
                here = (lane == CAP * j + r) & there
                late_task = jnp.where(here, task, late_task)
                late_tile = jnp.where(here, tile, late_tile)
        lists[0] = early
        lists[1] = late_task
        lists[2] = late_tile
        loads = [
            pltpu.make_async_copy(lists.at[n], ref, own_sem.at[n]) for n, ref in enumerate((ids_s, late_task_s, late_tile_s))
        ]
        for load in loads:
            load.start()
        for load in loads:
            load.wait()

    def late(ref, n):
        return ref[n // LATE_TASKS, n % LATE_TASKS]

    def list_late_groups():
        for g in range(LATE_GROUPS):
            rows = [buf_i[n // LATE_TASKS, late(late_task_s, n)] for n in range(g * GROUP, (g + 1) * GROUP)]
            hi, lo = split(jnp.concatenate(rows, axis=0).T)
            late_hi[g] = hi
            late_lo[g] = lo

    def dot(a, b):
        return lax.dot_general(a, b, (((1,), (0,)), ((), ())), preferred_element_type=jnp.float32)

    def product(tile_of, groups, b_hi, b_lo):
        def side(ref):
            return jnp.concatenate(
                [jnp.concatenate([ref[tile_of(g * GROUP + j)] for j in range(GROUP)], axis=0) for g in range(groups)], axis=1
            )

        a_hi, a_lo = side(amp_hi), side(amp_lo)
        b_hi = b_hi[...].reshape(groups * TW, GROUP * AB)
        b_lo = b_lo[...].reshape(groups * TW, GROUP * AB)
        return dot(a_hi, b_hi) + dot(a_lo, b_hi) + dot(a_hi, b_lo)

    for t in range(STEPS + LAG):
        arrived = [s for s in range(STEPS) if s + lag(s) == t]
        for s in arrived:
            for copy in sent[s].values():
                copy.wait_recv()
        if t < STEPS:
            for copy in sent.get(t - SEND_AGAIN, {}).values():
                copy.wait_send()
            sent[t] = {}
            for d in range(4):
                if TABLE[d][t] >= 0:
                    p, zb, xb = place(TABLE[d][t])
                    mine = amp.at[:, pl.ds(p * PT * TW, PT * TW)] if TABLE[d][t] % 64 == 0 else None
                    sent[t][d] = start(
                        buf_a.at[p, zb, xb], to[d], send_sem.at[d, t % SEND_AGAIN], recv_sem.at[d, t % RECV_AGAIN], mine
                    )
        for m in range(Y_MSGS):
            if Y_STEP[m] == t:
                y_send(m)
        if t == 0:
            number_tasks()
            block = buf_ids.at[o]
            sent_ids = [send(block, to_yr), send(block, to_yl), send(block, to_co)]
            amp_hi[N_TILES] = jnp.zeros((PAIRS, TW), jnp.bfloat16)
            amp_lo[N_TILES] = jnp.zeros((PAIRS, TW), jnp.bfloat16)
            for copy in own[4:]:
                copy.wait()
            for p in range(PARTS):
                convert_part(p, z, x)
        if t == 1:
            for q in range(0, Y_OWN, BATCH):
                to_core(t, o, q, BATCH, ints.at[pl.ds(q * Y_TASKS, BATCH * Y_TASKS)])
            own[3].wait()
            convert_groups(o, 0, SLOTS // GROUP)
        if t == LAG:
            sent_ids[0].wait_recv()
            sent_ids[1].wait_recv()
            sent_ids += [
                send(buf_ids.at[line(yl, c)], to_yr),
                send(buf_ids.at[line(yl, c)], to_co),
                send(buf_ids.at[line(yr, c)], to_co),
            ]
        if t == 2 * LAG:
            sent_ids[3].wait_recv()
            sent_ids.append(send(buf_ids.at[line(yo, c)], to_co))
        if t == 3 * LAG:
            for copy in [sent_ids[2]] + sent_ids[4:]:
                copy.wait_recv()
            list_tasks()
        for m in range(Y_MSGS):
            if Y_STEP[m] + LAG == t:
                y_arrived(t, m)
        for work in todo.pop(t, []):
            work()
        for s in arrived:
            for d in range(4):
                if TABLE[d][s] >= 0:
                    p, zb, xb = place(TABLE[d][s])
                    if d == 0:
                        xb = (xb + NX - 1) % NX
                    elif d == 1:
                        xb = (xb + 1) % NX
                    elif d == 2:
                        zb = (zb + NZ - 1) % NZ
                    else:
                        zb = (zb + 1) % NZ
                    convert_part(p, zb, xb)
        if t == LATE_READY:
            list_late_groups()
        if t == STEPS - LATE_STEPS - 1 + LAG:
            total[...] = product(lambda n: ids_s[n // SLOTS, n % SLOTS], N_GROUPS, int_hi, int_lo)

    total[...] += product(lambda n: late(late_tile_s, n), LATE_GROUPS, late_hi, late_lo)
    result = total[pl.ds(0, PAIRS), pl.ds(0, AB)]
    for j in range(1, GROUP):
        result = result + total[pl.ds(j * PAIRS, PAIRS), pl.ds(j * AB, AB)]
    out[...] = result
    left = [copy for t in range(STEPS - SEND_AGAIN, STEPS) for copy in sent[t].values()]
    left += [copy for m in range(Y_MSGS - Y_SEND_AGAIN, Y_MSGS) for copy in sent_y[m]]
    for copy in left + singles:
        copy.wait_send()


def body(amplitude, integrals, task_count, task_owner, task_local):
    f32, bf16 = jnp.float32, jnp.bfloat16
    return pl.pallas_call(
        kernel,
        out_shape=jax.ShapeDtypeStruct((PAIRS, AB), f32),
        in_specs=[pl.BlockSpec(memory_space=pltpu.HBM)] * 5,
        out_specs=pl.BlockSpec(memory_space=pltpu.VMEM),
        scratch_shapes=[
            pltpu.VMEM((PARTS, NZ, NX, PAIRS, PT * TW), f32),
            pltpu.VMEM((N_OCC, SLOTS, AB, TW), f32),
            pltpu.VMEM((N_OCC, 8, TW), jnp.int32),
            pltpu.SMEM((N_OCC, TW), jnp.int32),
            pltpu.SMEM((1, 1), jnp.int32),
            pltpu.VMEM((1, SLOTS), jnp.int32),
            pltpu.VMEM((1, SLOTS), jnp.int32),
            pltpu.VMEM((N_TILES + 1, PAIRS, TW), bf16),
            pltpu.VMEM((N_TILES + 1, PAIRS, TW), bf16),
            pltpu.VMEM((N_GROUPS, TW, GROUP * AB), bf16),
            pltpu.VMEM((N_GROUPS, TW, GROUP * AB), bf16),
            pltpu.VMEM((LATE_GROUPS, TW, GROUP * AB), bf16),
            pltpu.VMEM((LATE_GROUPS, TW, GROUP * AB), bf16),
            pltpu.VMEM((3, N_OCC, TW), jnp.int32),
            pltpu.SMEM((N_OCC, TW), jnp.int32),
            pltpu.SMEM((N_OCC, TW), jnp.int32),
            pltpu.VMEM((GROUP * PAIRS, GROUP * AB), f32),
            pltpu.SemaphoreType.DMA((4 + PARTS,)),
            pltpu.SemaphoreType.DMA((4, SEND_AGAIN)),
            pltpu.SemaphoreType.DMA((4, RECV_AGAIN)),
            pltpu.SemaphoreType.DMA((2, Y_SEND_AGAIN)),
            pltpu.SemaphoreType.DMA((2, Y_RECV_AGAIN)),
            pltpu.SemaphoreType.DMA((SINGLES,)),
            pltpu.SemaphoreType.DMA((SINGLES,)),
        ],
        compiler_params=pltpu.CompilerParams(
            collective_id=0, has_side_effects=True, vmem_limit_bytes=64 * 1024 * 1024
        ),
    )(
        amplitude,
        integrals[0, 0],
        task_count,
        task_owner.reshape(1, SLOTS),
        task_local.reshape(1, SLOTS),
    )


def solution(mesh):
    in_specs = (
        P("occ", "vir"),
        P("occ", "vir", None, None, None),
        P("occ", "vir"),
        P("occ", "vir", None, None),
        P("occ", "vir", None),
    )
    return jax.shard_map(body, mesh=mesh, in_specs=in_specs, out_specs=P("occ", "vir"), check_vma=False)
```

```python
import jax
import jax.numpy as jnp
from jax import lax
from jax.experimental import pallas as pl
from jax.experimental.pallas import tpu as pltpu
from jax.sharding import PartitionSpec as P

MESH = pl.DeviceIdType.MESH

NX, NY, NZ = 4, 4, 16
PAIRS = 16
TW = 128
TPD = 18
SLOTS = 64
AB = 32
N_OCC = 8
N_TILES = NX * NZ * TPD
GROUP = 8
N_GROUPS = N_OCC * SLOTS // GROUP

PARTS = 3
LAGS = (3, 3, 3, 4, 4, 5, 5, 5,)
LAG = LAGS[-1]
TABLE = (
    (0, 128, 64, 16, 144, 1, 143, 14, 130, 78, 142, 2, 30, 3, 13, 67, 141, 4, 132, 76, 68, 157, 140, 147, 11, 133, 139, 10, 69,
     91, 149, 74, 7, 135, 73, 71, 27, 25, 72, 89, 19, 158, 81, 175, 88, 23, 87, -1),
    (64, 0, 128, 112, 79, 65, 129, 2, 14, 127, 142, 177, 66, 131, 77, 141, 3, 114, 76, 125, 68, 140, 11, 75, 60, 116, 52, 6, 134,
     74, 70, 138, 54, 182, 187, 137, 135, 8, 136, 72, 185, 61, 1, 126, 184, 122, 183, 102),
    (0, 128, 64, 1, 129, 65, 80, 2, 130, 32, 66, 177, 3, 131, 81, 67, 146, 4, 132, 179, 68, 51, 5, 133, 180, 69, 52, 6, 134, 20,
     70, 100, 7, 135, 54, 118, 101, 33, 46, 151, 161, 144, 62, 36, 114, 41, 149, -1),
    (0, 64, 128, 15, 79, 143, 16, 14, 78, 127, 142, 160, 13, 77, 62, 141, 94, 12, 76, 61, 140, 29, 11, 75, 92, 139, 188, 10, 74,
     59, 138, 155, 26, 73, 58, 122, 154, 25, 100, 109, 173, 80, 165, 118, 41, 23, 171, -1),
)
STEPS = len(TABLE[0])
PT = TPD // PARTS
LATE_STEPS = 3
LATE = ((1, 6), (2, 7), (2, 10))
CAP = 2
LATE_TASKS = CAP * len(LATE)
LATE_GROUPS = N_OCC * LATE_TASKS // GROUP

Y_TASKS = 4
Y_OWN = SLOTS // Y_TASKS
Y_MSGS = Y_OWN + Y_OWN // 2
Y_STEP = [m * (STEPS - 12) // Y_MSGS for m in range(Y_MSGS)]
BATCH = 4
SEND_AGAIN, RECV_AGAIN = 6, 12
Y_SEND_AGAIN, Y_RECV_AGAIN = 6, 9
SINGLES = 23
LATE_READY = Y_STEP[-1] + 2 * LAG + 1


def lag(t):
    return LAGS[min(t, len(LAGS) - 1)]


def kernel(amp, ints, count_hbm, owner_hbm, local_hbm, out, buf_a, buf_i, buf_ids, ids_s, count_s, owner_v, local_v,
           amp_hi, amp_lo, int_hi, int_lo, late_hi, late_lo, lists, late_task_s, late_tile_s, total, own_sem, send_sem, recv_sem,
           y_send_sem, y_recv_sem, one_send_sem, one_recv_sem):
    o, v = lax.axis_index("occ"), lax.axis_index("vir")
    y, c = o // 2, o % 2
    x, z = v // NZ, v % NZ

    def at(yy, cc, xx, zz):
        return (yy * 2 + cc, xx * NZ + zz)

    def line(yy, cc):
        return yy * 2 + cc

    yr, yl, yo = (y + 1) % NY, (y + NY - 1) % NY, (y + 2) % NY
    to_yr, to_yl = at(yr, c, x, z), at(yl, c, x, z)
    to_co = at(y, 1 - c, x, z)
    to = (
        at(y, c, (x + 1) % NX, z),
        at(y, c, (x + NX - 1) % NX, z),
        at(y, c, x, (z + 1) % NZ),
        at(y, c, x, (z + NZ - 1) % NZ),
    )

    own = [
        pltpu.make_async_copy(count_hbm, count_s, own_sem.at[0]),
        pltpu.make_async_copy(owner_hbm, owner_v, own_sem.at[1]),
        pltpu.make_async_copy(local_hbm, local_v, own_sem.at[2]),
        pltpu.make_async_copy(ints, buf_i.at[o], own_sem.at[3]),
    ]
    for p in range(PARTS):
        own.append(pltpu.make_async_copy(amp.at[:, pl.ds(p * PT * TW, PT * TW)], buf_a.at[p, z, x], own_sem.at[4 + p]))
    for copy in own:
        copy.start()

    barrier = pltpu.get_barrier_semaphore()
    for device in (to_yr, to_yl, to_co) + to:
        pl.semaphore_signal(barrier, inc=1, device_id=device, device_id_type=MESH)

    def start(ref, device, send_one, recv_one, source=None):
        copy = pltpu.make_async_remote_copy(
            src_ref=ref if source is None else source, dst_ref=ref, send_sem=send_one, recv_sem=recv_one, device_id=device, device_id_type=MESH
        )
        copy.start()
        return copy

    singles = []

    def send(ref, device, source=None):
        n = len(singles)
        singles.append(start(ref, device, one_send_sem.at[n], one_recv_sem.at[n], source))
        return singles[n]

    def split(value):
        hi = value.astype(jnp.bfloat16)
        return hi, (value - hi.astype(jnp.float32)).astype(jnp.bfloat16)

    def place(code):
        p, dx, dz = code // 64, code // NZ % NX, code % NZ
        return p, (z + NZ - dz) % NZ, (x + NX - dx) % NX

    def convert_part(p, zb, xb):
        first = (xb * NZ + zb) * TPD + p * PT

        def one(t, carry):
            hi, lo = split(buf_a[p, zb, xb, :, pl.ds(pl.multiple_of(t * TW, TW), TW)])
            amp_hi[first + t] = hi
            amp_lo[first + t] = lo
            return carry

        lax.fori_loop(0, PT, one, 0, unroll=True)

    def convert_groups(oo, first, number):
        def one(j, carry):
            rows = buf_i[oo, pl.ds((first + j) * GROUP, GROUP)].reshape(GROUP * AB, TW)
            hi, lo = split(rows.T)
            g = oo * (SLOTS // GROUP) + first + j
            int_hi[g] = hi
            int_lo[g] = lo
            return carry

        lax.fori_loop(0, number, one, 0)

    def tasks(oo, m, number):
        return buf_i.at[oo, pl.ds(m * Y_TASKS, number * Y_TASKS)]

    pl.semaphore_wait(barrier, 7)

    def number_tasks():
        for copy in own[:3]:
            copy.wait()
        slot = lax.broadcasted_iota(jnp.int32, (1, SLOTS), 1)
        ids = jnp.where(slot < count_s[0, 0], owner_v[...] * TPD + local_v[...], N_TILES)
        buf_ids[o] = jnp.zeros((8, TW), jnp.int32)
        buf_ids[o, :, pl.ds(0, SLOTS)] = jnp.broadcast_to(ids, (8, SLOTS))

    sent, sent_y, sent_co, sent_ids = {}, {}, [], []
    todo = {}

    def later(t, work):
        todo.setdefault(t, []).append(work)

    def to_core(t, oo, m, number, source=None):
        copy = send(tasks(oo, m, number), to_co, source)
        other = oo + 1 - 2 * c

        def work():
            copy.wait_recv()
            convert_groups(other, m * Y_TASKS // GROUP, 1)

        later(t + LAG, work)
        later(t + LAG + 1, lambda: convert_groups(other, m * Y_TASKS // GROUP + 1, 1))

    def y_arrived(t, m):
        for copy in sent_y[m]:
            copy.wait_recv()
        end = m + 1
        pair = GROUP // Y_TASKS
        if end % pair == 0:
            if m < Y_OWN:
                for yy in (yl, yr):
                    convert_groups(line(yy, c), end // pair - 1, 1)
            else:
                for half in (0, Y_OWN // 2):
                    convert_groups(line(yo, c), (half + end - Y_OWN) // pair - 1, 1)
        if end % BATCH:
            return
        first = end - BATCH
        if m < Y_OWN:
            for yy in (yl, yr):
                to_core(t, line(yy, c), first, BATCH)
        else:
            for half in (0, Y_OWN // 2):
                to_core(t, line(yo, c), half + first - Y_OWN, BATCH)

    def y_send(m):
        if m >= Y_SEND_AGAIN:
            for copy in sent_y[m - Y_SEND_AGAIN]:
                copy.wait_send()
        if m < Y_OWN:
            right = left = tasks(o, m, 1)
            source = ints.at[pl.ds(m * Y_TASKS, Y_TASKS)]
        else:
            source = None
            right = tasks(line(yl, c), m - Y_OWN, 1)
            left = tasks(line(yr, c), Y_OWN // 2 + m - Y_OWN, 1)
        sent_y[m] = [
            start(ref, device, y_send_sem.at[d, m % Y_SEND_AGAIN], y_recv_sem.at[d, m % Y_RECV_AGAIN], source)
            for d, (ref, device) in enumerate(((right, to_yr), (left, to_yl)))
        ]

    def list_tasks():
        ids = jnp.concatenate([buf_ids[oo, pl.ds(0, 1), :] for oo in range(N_OCC)], axis=0)
        lane = lax.broadcasted_iota(jnp.int32, (N_OCC, TW), 1)
        early, late_task, late_tile = ids, jnp.zeros((N_OCC, TW), jnp.int32), jnp.full((N_OCC, TW), N_TILES, jnp.int32)
        for j, (dx, dz) in enumerate(LATE):
            first = ((x + NX - dx) % NX * NZ + (z + NZ - dz) % NZ) * TPD
            named = (ids >= first) & (ids < first + TPD) & (lane < SLOTS)
            early = jnp.where(named, N_TILES, early)
            low = jnp.min(jnp.where(named, lane, TW), axis=1, keepdims=True)
            high = jnp.max(jnp.where(named, lane, -1), axis=1, keepdims=True)
            for r, (task, there) in enumerate(((low, low < TW), (high, high > low))):
                tile = jnp.sum(jnp.where(named & (lane == task), ids, 0), axis=1, keepdims=True)
                here = (lane == CAP * j + r) & there
                late_task = jnp.where(here, task, late_task)
                late_tile = jnp.where(here, tile, late_tile)
        lists[0] = early
        lists[1] = late_task
        lists[2] = late_tile
        loads = [
            pltpu.make_async_copy(lists.at[n], ref, own_sem.at[n]) for n, ref in enumerate((ids_s, late_task_s, late_tile_s))
        ]
        for load in loads:
            load.start()
        for load in loads:
            load.wait()

    def late(ref, n):
        return ref[n // LATE_TASKS, n % LATE_TASKS]

    def list_late_groups():
        for g in range(LATE_GROUPS):
            rows = [buf_i[n // LATE_TASKS, late(late_task_s, n)] for n in range(g * GROUP, (g + 1) * GROUP)]
            hi, lo = split(jnp.concatenate(rows, axis=0).T)
            late_hi[g] = hi
            late_lo[g] = lo

    def dot(a, b):
        return lax.dot_general(a, b, (((1,), (0,)), ((), ())), preferred_element_type=jnp.float32)

    def product(tile_of, groups, b_hi, b_lo):
        def side(ref):
            return jnp.concatenate(
                [jnp.concatenate([ref[tile_of(g * GROUP + j)] for j in range(GROUP)], axis=0) for g in range(groups)], axis=1
            )

        a_hi, a_lo = side(amp_hi), side(amp_lo)
        b_hi = b_hi[...].reshape(groups * TW, GROUP * AB)
        b_lo = b_lo[...].reshape(groups * TW, GROUP * AB)
        return dot(a_hi, b_hi) + dot(a_lo, b_hi) + dot(a_hi, b_lo)

    for t in range(STEPS + LAG):
        arrived = [s for s in range(STEPS) if s + lag(s) == t]
        for s in arrived:
            for copy in sent[s].values():
                copy.wait_recv()
        if t < STEPS:
            for copy in sent.get(t - SEND_AGAIN, {}).values():
                copy.wait_send()
            sent[t] = {}
            for d in range(4):
                if TABLE[d][t] >= 0:
                    p, zb, xb = place(TABLE[d][t])
                    mine = amp.at[:, pl.ds(p * PT * TW, PT * TW)] if TABLE[d][t] % 64 == 0 else None
                    sent[t][d] = start(
                        buf_a.at[p, zb, xb], to[d], send_sem.at[d, t % SEND_AGAIN], recv_sem.at[d, t % RECV_AGAIN], mine
                    )
        for m in range(Y_MSGS):
            if Y_STEP[m] == t:
                y_send(m)
        if t == 0:
            number_tasks()
            block = buf_ids.at[o]
            sent_ids = [send(block, to_yr), send(block, to_yl), send(block, to_co)]
            amp_hi[N_TILES] = jnp.zeros((PAIRS, TW), jnp.bfloat16)
            amp_lo[N_TILES] = jnp.zeros((PAIRS, TW), jnp.bfloat16)
            for copy in own[4:]:
                copy.wait()
            for p in range(PARTS):
                convert_part(p, z, x)
        if t == 1:
            for q in range(0, Y_OWN, BATCH):
                to_core(t, o, q, BATCH, ints.at[pl.ds(q * Y_TASKS, BATCH * Y_TASKS)])
            own[3].wait()
        if 2 <= t < 2 + SLOTS // GROUP:
            convert_groups(o, t - 2, 1)
        if t == LAG:
            sent_ids[0].wait_recv()
            sent_ids[1].wait_recv()
            sent_ids += [
                send(buf_ids.at[line(yl, c)], to_yr),
                send(buf_ids.at[line(yl, c)], to_co),
                send(buf_ids.at[line(yr, c)], to_co),
            ]
        if t == 2 * LAG:
            sent_ids[3].wait_recv()
            sent_ids.append(send(buf_ids.at[line(yo, c)], to_co))
        if t == 3 * LAG:
            for copy in [sent_ids[2]] + sent_ids[4:]:
                copy.wait_recv()
            list_tasks()
        for m in range(Y_MSGS):
            if Y_STEP[m] + LAG == t:
                y_arrived(t, m)
        for work in todo.pop(t, []):
            work()
        for s in arrived:
            for d in range(4):
                if TABLE[d][s] >= 0:
                    p, zb, xb = place(TABLE[d][s])
                    if d == 0:
                        xb = (xb + NX - 1) % NX
                    elif d == 1:
                        xb = (xb + 1) % NX
                    elif d == 2:
                        zb = (zb + NZ - 1) % NZ
                    else:
                        zb = (zb + 1) % NZ
                    convert_part(p, zb, xb)
        if t == LATE_READY:
            list_late_groups()
        if t == STEPS - LATE_STEPS - 1 + LAG:
            total[...] = product(lambda n: ids_s[n // SLOTS, n % SLOTS], N_GROUPS, int_hi, int_lo)

    total[...] += product(lambda n: late(late_tile_s, n), LATE_GROUPS, late_hi, late_lo)
    result = total[pl.ds(0, PAIRS), pl.ds(0, AB)]
    for j in range(1, GROUP):
        result = result + total[pl.ds(j * PAIRS, PAIRS), pl.ds(j * AB, AB)]
    out[...] = result
    left = [copy for t in range(STEPS - SEND_AGAIN, STEPS) for copy in sent[t].values()]
    left += [copy for m in range(Y_MSGS - Y_SEND_AGAIN, Y_MSGS) for copy in sent_y[m]]
    for copy in left + singles:
        copy.wait_send()


def body(amplitude, integrals, task_count, task_owner, task_local):
    f32, bf16 = jnp.float32, jnp.bfloat16
    return pl.pallas_call(
        kernel,
        out_shape=jax.ShapeDtypeStruct((PAIRS, AB), f32),
        in_specs=[pl.BlockSpec(memory_space=pltpu.HBM)] * 5,
        out_specs=pl.BlockSpec(memory_space=pltpu.VMEM),
        scratch_shapes=[
            pltpu.VMEM((PARTS, NZ, NX, PAIRS, PT * TW), f32),
            pltpu.VMEM((N_OCC, SLOTS, AB, TW), f32),
            pltpu.VMEM((N_OCC, 8, TW), jnp.int32),
            pltpu.SMEM((N_OCC, TW), jnp.int32),
            pltpu.SMEM((1, 1), jnp.int32),
            pltpu.VMEM((1, SLOTS), jnp.int32),
            pltpu.VMEM((1, SLOTS), jnp.int32),
            pltpu.VMEM((N_TILES + 1, PAIRS, TW), bf16),
            pltpu.VMEM((N_TILES + 1, PAIRS, TW), bf16),
            pltpu.VMEM((N_GROUPS, TW, GROUP * AB), bf16),
            pltpu.VMEM((N_GROUPS, TW, GROUP * AB), bf16),
            pltpu.VMEM((LATE_GROUPS, TW, GROUP * AB), bf16),
            pltpu.VMEM((LATE_GROUPS, TW, GROUP * AB), bf16),
            pltpu.VMEM((3, N_OCC, TW), jnp.int32),
            pltpu.SMEM((N_OCC, TW), jnp.int32),
            pltpu.SMEM((N_OCC, TW), jnp.int32),
            pltpu.VMEM((GROUP * PAIRS, GROUP * AB), f32),
            pltpu.SemaphoreType.DMA((4 + PARTS,)),
            pltpu.SemaphoreType.DMA((4, SEND_AGAIN)),
            pltpu.SemaphoreType.DMA((4, RECV_AGAIN)),
            pltpu.SemaphoreType.DMA((2, Y_SEND_AGAIN)),
            pltpu.SemaphoreType.DMA((2, Y_RECV_AGAIN)),
            pltpu.SemaphoreType.DMA((SINGLES,)),
            pltpu.SemaphoreType.DMA((SINGLES,)),
        ],
        compiler_params=pltpu.CompilerParams(
            collective_id=0, has_side_effects=True, vmem_limit_bytes=64 * 1024 * 1024
        ),
    )(
        amplitude,
        integrals[0, 0],
        task_count,
        task_owner.reshape(1, SLOTS),
        task_local.reshape(1, SLOTS),
    )


def solution(mesh):
    in_specs = (
        P("occ", "vir"),
        P("occ", "vir", None, None, None),
        P("occ", "vir"),
        P("occ", "vir", None, None),
        P("occ", "vir", None),
    )
    return jax.shard_map(body, mesh=mesh, in_specs=in_specs, out_specs=P("occ", "vir"), check_vma=False)
```
